512 devices in a mesh: lat: 16 (over x_hi, y, core), lon: 32 (over z, x_lo).
Axes of the slice: x: 4 (x_hi: 2, x_lo: 2; x = x_hi * 2 + x_lo), y: 4, z: 16, core: 2. Of those that a mesh axis runs over, the one named last changes fastest.
Arguments:
- fields: bfloat16 [32, 256, 8192], P('lon', 'lat'), may hold values from -6 to 6
- weight: bfloat16 [64, 32, 3, 3], replicated, may hold values from -0.375 to 0.375
- bias: float32 [64], replicated, may hold values from -3 to 3
- land_bias: float32 [64], replicated, may hold values from -4 to 4
- land_mask: int32 [256, 8192], P('lat', 'lon'), may hold values 0 or 1
- cotangent: bfloat16 [64, 128, 4096], P(None, 'lat', 'lon'), may hold values from -6 to 6
Outputs:
- pooled: bfloat16 [64, 128, 4096], P(None, 'lat', 'lon')
- grad_weight: float32 [64, 32, 3, 3], replicated
- grad_bias: float32 [64], replicated
- grad_land: float32 [64], replicated
The draws below stay inside these ranges and needn't reach their ends.
All inputs are finite; a program needn't handle non-finite values. No bound on the sum of `land_mask` on one device may be relied on, other than what follows from the above.
Results may differ from the reference program's by a relative error of at most 0.0029.
Values may be sent and summed in bfloat16 or wider, within the bound.
No kernel may reach another device: no remote copies, remote signals or barrier semaphores. Data moves between devices by JAX's collectives and lax.ppermute only.
A program may use at most 64 MiB of HBM per device.

```python
import math
import jax
import jax.numpy as jnp
from jax import lax

FIELDS = 32
CH = 64
NLAT = 256
NLON = 8192


def plant(drawn, key, smallest, largest):
    place = [jax.random.randint(jax.random.fold_in(key, axis), (), 0, length) for axis, length in enumerate(drawn.shape)]
    widest = drawn.shape.index(max(drawn.shape))
    neighbour = place[:widest] + [(place[widest] + 1) % drawn.shape[widest]] + place[widest + 1:]
    return drawn.at[tuple(place)].set(smallest).at[tuple(neighbour)].set(largest)


def shard_levels(stream_key, dims, cuts, least, largest):
    def one(dim, parts):
        heights = jax.random.uniform(jax.random.fold_in(jax.random.fold_in(stream_key, 6), dim), (parts,), jnp.float32, least / len(cuts), largest / len(cuts))
        return jnp.repeat(jnp.exp(heights), dims[dim] // parts).reshape((-1,) + (1,) * (len(dims) - dim - 1))

    loudness = one(*cuts[0])
    for cut in cuts[1:]:
        loudness = loudness * one(*cut)
    return loudness


def normal_values(stream_key, extent, spread, bound, cuts=(), held_as=jnp.bfloat16):
    array = spread * jax.random.normal(stream_key, extent, jnp.float32)
    if cuts:
        array = array * shard_levels(stream_key, extent, cuts, -0.22, 0.18)
    return jnp.clip(array, -bound, bound).astype(held_as)


def setup_inputs(seed: int = 0) -> dict:
    arg_keys = jax.random.split(jax.random.key(seed), 7)
    fields = normal_values(arg_keys[0], (FIELDS, NLAT, NLON), 1.0, 6.0, ((0, 32), (1, 16)))
    weight = normal_values(arg_keys[1], (CH, FIELDS, 3, 3), (FIELDS * 9) ** -0.5, 0.375)
    bias = normal_values(arg_keys[2], (CH,), 0.5, 3.0, (), jnp.float32)
    land_bias = normal_values(arg_keys[3], (CH,), 1.0, 4.0, (), jnp.float32)
    land_mask = plant((jax.random.randint(arg_keys[4], (NLAT, NLON), 0, 10) < 3).astype(jnp.int32), jax.random.fold_in(arg_keys[4], 1), 0, 1)
    cotangent = normal_values(arg_keys[5], (CH, NLAT // 2, NLON // 2), 1.0, 6.0, ((1, 16), (2, 32)))
    return dict(fields=fields, weight=weight, bias=bias, land_bias=land_bias, land_mask=land_mask, cotangent=cotangent)


def pad_grid(fields):
    zero_row = jnp.zeros((fields.shape[0], 1, fields.shape[2]), fields.dtype)
    lat_padded = jnp.concatenate([zero_row, fields, zero_row], axis=1)
    return jnp.concatenate([lat_padded[:, :, -1:], lat_padded, lat_padded[:, :, :1]], axis=2)

def reference(fields, weight, bias, land_bias, land_mask, cotangent):
    padded = pad_grid(fields)
    block_rows = math.gcd(NLAT, 16)
    block_count = NLAT // block_rows
    scale = 1.0 / math.sqrt(NLAT * NLON / 4.0)
    weight_f = weight.astype(jnp.float32)

    def one_block(carry, index):
        grad_w, grad_b, grad_l = carry
        start = (index * block_rows).astype(jnp.int32)
        slab = lax.dynamic_slice_in_dim(padded, start, block_rows + 2, 1).astype(jnp.float32)
        mask_rows = lax.dynamic_slice_in_dim(land_mask, start, block_rows, 0).astype(jnp.float32)
        cot_rows = lax.dynamic_slice_in_dim(cotangent, (index * (block_rows // 2)).astype(jnp.int32), block_rows // 2, 1)
        preact = bias[:, None, None] + land_bias[:, None, None] * mask_rows[None]
        for row_off in range(3):
            for col_off in range(3):
                window = slab[:, row_off:row_off + block_rows, col_off:col_off + NLON]
                preact = preact + jnp.einsum('oc,chw->ohw', weight_f[:, :, row_off, col_off], window)
        activated, pullback = jax.vjp(jax.nn.gelu, preact)
        pooled_rows = (activated.reshape(CH, block_rows // 2, 2, NLON // 2, 2).sum(axis=(2, 4)) * 0.25).astype(jnp.bfloat16)
        scaled = cot_rows.astype(jnp.float32) * (scale * 0.25)
        grad_act = jnp.repeat(jnp.repeat(scaled, 2, axis=1), 2, axis=2)
        grad_pre = pullback(grad_act)[0]
        grad_low = grad_pre.astype(jnp.bfloat16).astype(jnp.float32)
        pieces = []
        for row_off in range(3):
            across = []
            for col_off in range(3):
                window = slab[:, row_off:row_off + block_rows, col_off:col_off + NLON]
                across.append(jnp.einsum('ohw,chw->oc', grad_low, window))
            pieces.append(jnp.stack(across, axis=-1))
        grad_w = grad_w + jnp.stack(pieces, axis=-2)
        grad_b = grad_b + grad_pre.sum(axis=(1, 2))
        grad_l = grad_l + (grad_pre * mask_rows[None]).sum(axis=(1, 2))
        return ((grad_w, grad_b, grad_l), pooled_rows)
    start_carry = (jnp.zeros((CH, FIELDS, 3, 3), jnp.float32), jnp.zeros((CH,), jnp.float32), jnp.zeros((CH,), jnp.float32))
    totals, pooled_blocks = lax.scan(one_block, start_carry, jnp.arange(block_count, dtype=jnp.int32))
    pooled = jnp.transpose(pooled_blocks, (1, 0, 2, 3)).reshape(CH, NLAT // 2, NLON // 2)
    return (pooled, totals[0], totals[1], totals[2])
```

```python
import functools
import math

import jax
import jax.numpy as jnp
from jax import lax
from jax.experimental import pallas as pl
from jax.experimental.pallas import tpu as pltpu
from jax.sharding import Mesh
from jax.sharding import PartitionSpec as P

AXES = ("xh", "y", "c", "z", "xl")
LAT = ("xh", "y", "c")
LON = ("z", "xl")
PLANE = ("xh", "xl", "y", "c")
F32 = jnp.float32
BF16 = jnp.bfloat16
ROWS = 16
COLS = 256
LANES = 128
PIECE = 40
VMEM = pl.BlockSpec(memory_space=pltpu.VMEM)


def iota(shape, dim):
    return lax.broadcasted_iota(jnp.int32, shape, dim)


def pack_kernel(tiles, x_ref, top_ref, bottom_ref, out_ref):
    rows8 = iota((8, LANES), 0)
    lanes = iota((24, LANES), 1)
    edges = jnp.zeros((24, LANES), F32)
    tails = []
    for tile in range(tiles):
        blocks = []
        for half in range(2):
            at = pl.ds(tile * COLS + half * LANES, LANES)
            body = x_ref[:, at]
            out_ref[tile, half * ROWS : (half + 1) * ROWS, :] = body
            top = top_ref[:, at].astype(F32)
            bottom = bottom_ref[:, at].astype(F32)
            blocks.append((top, bottom))
            halo = jnp.where(rows8 == 0, top, jnp.where(rows8 == 1, bottom, 0.0))
            block = jnp.concatenate([body.astype(F32), halo], axis=0)
            if half == 0:
                source, target = 0, 64 + (tile - 1) % tiles
            else:
                source, target = LANES - 1, (tile + 1) % tiles
            turned = pltpu.roll(block, (target - source) % LANES, 1)
            edges = jnp.where(lanes == target, turned, edges)
        tails.append(blocks)
    square = jnp.concatenate([edges, jnp.zeros((LANES - 24, LANES), F32)], axis=0).T
    columns = square[:tiles] + pltpu.roll(square[64 : 64 + tiles], 64, 1)
    for tile, ((top0, bottom0), (top1, bottom1)) in enumerate(tails):
        tail = jnp.where(rows8 == 0, top0, 0.0)
        tail = jnp.where(rows8 == 1, top1, tail)
        tail = jnp.where(rows8 == 2, bottom0, tail)
        tail = jnp.where(rows8 == 3, bottom1, tail)
        tail = jnp.where(rows8 == 4, columns[tile : tile + 1], tail)
        out_ref[tile, 2 * ROWS : PIECE, :] = tail.astype(BF16)


def column_of(row, count):
    return jnp.sum(jnp.where(iota((count, count), 0) == iota((count, count), 1), row, 0.0), axis=1, keepdims=True)


def conv_kernel(
    factor, r_ref, w_ref, bias_ref, land_ref, mask_ref, cot_ref, pooled_ref, sums_ref, flat_ref, patch_ref, wide0, wide1, act0, act1
):
    fields = r_ref.shape[0]
    channels = w_ref.shape[1]
    taps = 9 * fields
    pool_rows = ROWS // 2
    for c in range(fields):
        flat_ref[c * PIECE : (c + 1) * PIECE, :] = r_ref[c].astype(F32)

    def take(k):
        return flat_ref[pl.ds(k, fields, stride=PIECE), :]

    columns = take(36)
    col = iota((fields, COLS), 1)
    for r in range(ROWS + 2):
        if r == 0:
            first, second, lane = 32, 33, 16
        elif r == ROWS + 1:
            first, second, lane = 34, 35, 17
        else:
            first, second, lane = r - 1, ROWS + r - 1, r - 1
        x = jnp.concatenate([take(first), take(second)], axis=1)
        left = jnp.where(col == 0, columns[:, lane : lane + 1], pltpu.roll(x, 1, 1))
        right = jnp.where(col == COLS - 1, columns[:, 64 + lane : 65 + lane], pltpu.roll(x, COLS - 1, 1))
        patch_ref[r, 0:fields, :] = left.astype(BF16)
        patch_ref[r, fields : 2 * fields, :] = x.astype(BF16)
        patch_ref[r, 2 * fields : 3 * fields, :] = right.astype(BF16)

    weight = w_ref[...].astype(F32).T.astype(BF16)
    bias = column_of(bias_ref[...], channels)
    land = column_of(land_ref[...], channels)
    spread = (iota((LANES, COLS), 1) // 2 == iota((LANES, COLS), 0)).astype(F32).astype(BF16)
    wide = jnp.dot(cot_ref[...].reshape(channels * pool_rows, LANES), spread, preferred_element_type=F32) * factor
    wide0[...] = wide[:, :LANES]
    wide1[...] = wide[:, LANES:]

    root = math.sqrt(2.0 / math.pi)
    grad_w = jnp.zeros((taps, channels), F32)
    grad_b = jnp.zeros((channels, COLS), F32)
    grad_l = jnp.zeros((channels, COLS), F32)
    for p in range(pool_rows):
        here = pl.ds(p, channels, stride=pool_rows)
        grad_act = jnp.concatenate([wide0[here, :], wide1[here, :]], axis=1)
        act = None
        for i in (2 * p, 2 * p + 1):
            patch = patch_ref[i : i + 3].reshape(taps, COLS)
            mask = mask_ref[i : i + 1, :].astype(F32)
            v = jnp.dot(weight, patch, preferred_element_type=F32) + (bias + land * mask)
            square = v * v
            t = jnp.tanh(v * (root + (root * 0.044715) * square))
            half = 0.5 + 0.5 * t
            gelu = v * half
            slope = half + gelu * (1.0 - t) * (root + (3.0 * root * 0.044715) * square)
            grad_pre = grad_act * slope
            grad_w += lax.dot_general(
                patch, grad_pre.astype(BF16), (((1,), (1,)), ((), ())), preferred_element_type=F32
            )
            grad_b += grad_pre
            grad_l += grad_pre * mask
            act = gelu if act is None else act + gelu
        act0[here, :] = act[:, :LANES]
        act1[here, :] = act[:, LANES:]

    pair = (iota((COLS, LANES), 0) // 2 == iota((COLS, LANES), 1)).astype(F32).astype(BF16)
    total = jnp.concatenate([act0[...], act1[...]], axis=1)
    high = total.astype(BF16)
    low = (total - high.astype(F32)).astype(BF16)
    pooled = jnp.dot(high, pair, preferred_element_type=F32) + jnp.dot(low, pair, preferred_element_type=F32)
    pooled_ref[...] = (pooled * 0.25).astype(BF16).reshape(pooled_ref.shape)

    ones = jnp.ones((8, COLS), F32)

    def across(grad):
        return lax.dot_general(
            ones, grad, (((1,), (1,)), ((), ())), precision=lax.Precision.HIGHEST, preferred_element_type=F32
        )

    half_taps = taps // 2
    used = half_taps // 8
    sums_ref[0:used] = jnp.concatenate([grad_w[:half_taps], grad_w[half_taps:]], axis=1).reshape(used, 8, LANES)
    sums_ref[used] = jnp.concatenate([across(grad_b), across(grad_l)], axis=1)
    sums_ref[used + 1 :] = jnp.zeros((sums_ref.shape[0] - used - 1, 8, LANES), F32)


def sum_kernel(x_ref, out_ref):
    out_ref[...] = jnp.broadcast_to(jnp.sum(x_ref[...], axis=0, keepdims=True), out_ref.shape)


def unpack_kernel(x_ref, weight_ref, bias_ref, land_ref):
    half_taps = weight_ref.shape[0] // 2
    channels = weight_ref.shape[1]
    used = half_taps // 8
    both = x_ref[0:used].reshape(half_taps, LANES)
    weight_ref[0:half_taps, :] = both[:, :channels]
    weight_ref[half_taps:, :] = both[:, channels:]
    bias_ref[...] = x_ref[used, 0:1, :channels]
    land_ref[...] = x_ref[used, 0:1, channels:]


def call(kernel, name, outs, *args, scratch=(), flops=0):
    shapes = [jax.ShapeDtypeStruct(*o) for o in outs]
    single = len(shapes) == 1
    return pl.pallas_call(
        kernel,
        name=name,
        out_shape=shapes[0] if single else shapes,
        in_specs=[VMEM] * len(args),
        out_specs=VMEM if single else [VMEM] * len(shapes),
        scratch_shapes=list(scratch),
        compiler_params=pltpu.CompilerParams(vmem_limit_bytes=32 * 1024 * 1024),
    )(*args)


def local(fields, weight, bias, land_bias, land_mask, cotangent):
    channels, in_fields = weight.shape[:2]
    taps = 9 * in_fields
    tiles = lax.axis_size(LON)
    rows_count = lax.axis_size(LAT)
    field = fields[0]
    up = [(i, i + 1) for i in range(rows_count - 1)]
    down = [(i + 1, i) for i in range(rows_count - 1)]
    top = lax.ppermute(field[ROWS - 1 :], LAT, up)
    bottom = lax.ppermute(field[:1], LAT, down)
    pieces = call(
        functools.partial(pack_kernel, tiles), "pack", [((tiles, PIECE, LANES), BF16)], field, top, bottom
    )
    pieces = lax.all_to_all(pieces, LON, 0, 0, tiled=True)
    factor = 0.25 / math.sqrt(float(cotangent.shape[1] * rows_count * cotangent.shape[2] * tiles))
    members = lax.axis_size(PLANE)
    pooled, sums = call(
        functools.partial(conv_kernel, factor),
        "conv",
        [(cotangent.shape, BF16), ((members, 8, LANES), F32)],
        pieces,
        weight.transpose(2, 3, 1, 0).reshape(taps, channels),
        bias.reshape(1, channels),
        land_bias.reshape(1, channels),
        land_mask,
        cotangent,
        scratch=[
            pltpu.VMEM((in_fields * PIECE, LANES), F32),
            pltpu.VMEM((ROWS + 2, 3 * in_fields, COLS), BF16),
        ]
        + [pltpu.VMEM((channels * ROWS // 2, LANES), F32)] * 4,
    )
    sums = lax.all_to_all(sums, PLANE, 0, 0, tiled=True)
    sums = call(sum_kernel, "sum_plane", [((lax.axis_size("z"), 8, LANES), F32)], sums)
    sums = lax.all_to_all(sums, "z", 0, 0, tiled=True)
    sums = call(sum_kernel, "sum_z", [((members, 8, LANES), F32)], sums)
    sums = lax.all_to_all(sums, PLANE, 0, 0, tiled=True)
    grad_weight, grad_bias, grad_land = call(
        unpack_kernel,
        "unpack",
        [((taps, channels), F32), ((1, channels), F32), ((1, channels), F32)],
        sums,
    )
    grad_weight = grad_weight.reshape(3, 3, in_fields, channels).transpose(3, 2, 0, 1)
    return pooled, grad_weight, grad_bias.reshape(channels), grad_land.reshape(channels)


def solution(mesh):
    physical = Mesh(mesh.devices.reshape(2, 4, 2, 16, 2), AXES)
    placed = (P(LON, LAT, None), P(), P(), P(), P(LAT, LON), P(None, LAT, LON))
    return jax.shard_map(
        local,
        mesh=physical,
        in_specs=placed,
        out_specs=(P(None, LAT, LON), P(), P(), P()),
        check_vma=False,
    )
```

```python
import functools
import math

import jax
import jax.numpy as jnp
from jax import lax
from jax.experimental import pallas as pl
from jax.experimental.pallas import tpu as pltpu
from jax.sharding import Mesh
from jax.sharding import PartitionSpec as P

AXES = ("xh", "y", "c", "z", "xl")
LAT = ("xh", "y", "c")
LON = ("z", "xl")
PLANE = ("xh", "xl", "y", "c")
F32 = jnp.float32
BF16 = jnp.bfloat16
ROWS = 16
COLS = 256
LANES = 128
PIECE = 40
VMEM = pl.BlockSpec(memory_space=pltpu.VMEM)
ANY = pl.BlockSpec(memory_space=pl.ANY)
HBM = pl.BlockSpec(memory_space=pltpu.HBM)
SMEM = pl.BlockSpec(memory_space=pltpu.SMEM)


def iota(shape, dim):
    return lax.broadcasted_iota(jnp.int32, shape, dim)


def edge_lanes(tiles, tile, half):
    if half == 0:
        return 0, 64 + (tile - 1) % tiles
    return LANES - 1, (tile + 1) % tiles


def pack_kernel(tiles, core_ref, x_ref, outer_ref, inner_ref, edges_ref, out_ref):
    first = core_ref[0] == 0
    rows8 = iota((8, LANES), 0)
    lanes = iota((8, LANES), 1)
    beside = jnp.zeros((8, LANES), F32)
    tails = []
    for tile in range(tiles):
        for half in range(2):
            k = 2 * tile + half
            at = pl.ds(k * LANES, LANES)
            out_ref[tile, half * ROWS : (half + 1) * ROWS, :] = x_ref[:, at]
            outer = outer_ref[:, at].astype(F32)
            top = jnp.where(first, outer, inner_ref[k : k + 1, :])
            bottom = jnp.where(first, inner_ref[2 * tiles + k : 2 * tiles + k + 1, :], outer)
            tails.append((top, bottom))
            halo = jnp.where(rows8 == 0, top, jnp.where(rows8 == 1, bottom, 0.0))
            source, target = edge_lanes(tiles, tile, half)
            beside = jnp.where(lanes == target, pltpu.roll(halo, (target - source) % LANES, 1), beside)
    square = jnp.concatenate([edges_ref[...], beside, jnp.zeros((LANES - ROWS - 8, LANES), F32)], axis=0).T
    columns = square[:tiles] + pltpu.roll(square[64 : 64 + tiles], 64, 1)
    for tile in range(tiles):
        (top0, bottom0), (top1, bottom1) = tails[2 * tile : 2 * tile + 2]
        tail = jnp.where(rows8 == 0, top0, 0.0)
        tail = jnp.where(rows8 == 1, top1, tail)
        tail = jnp.where(rows8 == 2, bottom0, tail)
        tail = jnp.where(rows8 == 3, bottom1, tail)
        tail = jnp.where(rows8 == 4, columns[tile : tile + 1], tail)
        out_ref[tile, 2 * ROWS : PIECE, :] = tail.astype(BF16)


def column_of(row, count):
    return jnp.sum(jnp.where(iota((count, count), 0) == iota((count, count), 1), row, 0.0), axis=1, keepdims=True)


def edges_of(tiles, first, x_ref, outer_ref, inner_ref, edges_ref):
    lanes = iota((ROWS, LANES), 1)
    edges = jnp.zeros((ROWS, LANES), F32)
    for k in range(2 * tiles):
        at = pl.ds(k * LANES, LANES)
        block = x_ref[:, at].astype(F32)
        top, bottom = block[0:1], block[ROWS - 1 : ROWS]
        outer_ref[:, at] = jnp.where(first, top, bottom).astype(BF16)
        inner_ref[k : k + 1, :] = jnp.where(first, bottom, top)
        source, target = edge_lanes(tiles, k // 2, k % 2)
        edges = jnp.where(lanes == target, pltpu.roll(block, (target - source) % LANES, 1), edges)
    edges_ref[...] = edges


def first_kernel(
    tiles,
    factor,
    core_ref,
    x_in,
    w_in,
    bias_in,
    land_in,
    mask_in,
    cot_in,
    x_ref,
    outer_ref,
    inner_ref,
    edges_ref,
    w_out,
    bias_out,
    land_out,
    mask_out,
    wide_out,
    w_ref,
    bias_ref,
    land_ref,
    mask_ref,
    cot_ref,
    wide0,
    wide1,
    sems,
):
    pairs = [(x_in, x_ref), (cot_in, cot_ref), (w_in, w_ref), (bias_in, bias_ref), (land_in, land_ref), (mask_in, mask_ref)]
    copies = [pltpu.make_async_copy(source, target, sems.at[k]) for k, (source, target) in enumerate(pairs)]
    for copy in copies:
        copy.start()
    copies[0].wait()
    edges_of(tiles, core_ref[0] == 0, x_ref, outer_ref, inner_ref, edges_ref)
    for copy in copies[1:]:
        copy.wait()
    taps, channels = w_ref.shape
    pool_rows = ROWS // 2
    weight = w_ref[...].astype(F32).T
    zero = jnp.zeros((channels, taps // 3), F32)
    upper = jnp.concatenate([weight, zero], axis=1)
    lower = jnp.concatenate([zero, weight], axis=1)
    w_out[...] = jnp.concatenate([upper, lower], axis=0).astype(BF16)
    bias_out[...] = jnp.broadcast_to(column_of(bias_ref[...], channels), bias_out.shape)
    land_out[...] = jnp.broadcast_to(column_of(land_ref[...], channels), land_out.shape)
    mask_out[...] = mask_ref[...].astype(F32)
    spread = (iota((LANES, COLS), 1) // 2 == iota((LANES, COLS), 0)).astype(F32).astype(BF16)
    wide = jnp.dot(cot_ref[...].reshape(channels * pool_rows, LANES), spread, preferred_element_type=F32) * factor
    wide0[...] = wide[:, :LANES]
    wide1[...] = wide[:, LANES:]
    for p in range(pool_rows):
        here = pl.ds(p, channels, stride=pool_rows)
        wide_out[p] = jnp.concatenate([wide0[here, :], wide1[here, :]], axis=1)


def conv_kernel(r_ref, w_ref, bias_ref, land_ref, mask_ref, wide_ref, pooled_ref, sums_ref, flat_ref, patch_ref, low_ref, act0, act1, pooled_vmem, sem):
    fields = r_ref.shape[0]
    channels = bias_ref.shape[0]
    taps = 9 * fields
    pool_rows = ROWS // 2
    for c in range(fields):
        flat_ref[c * PIECE : (c + 1) * PIECE, :] = r_ref[c].astype(F32)

    def take(k):
        return flat_ref[pl.ds(k, fields, stride=PIECE), :]

    columns = take(36)
    first_lane = iota((fields, LANES), 1) == 0
    last_lane = iota((fields, LANES), 1) == LANES - 1
    for r in range(ROWS + 2):
        if r == 0:
            k0, k1, lane = 32, 33, 16
        elif r == ROWS + 1:
            k0, k1, lane = 34, 35, 17
        else:
            k0, k1, lane = r - 1, ROWS + r - 1, r - 1
        a, b = take(k0), take(k1)
        up_a, up_b = pltpu.roll(a, 1, 1), pltpu.roll(b, 1, 1)
        down_a, down_b = pltpu.roll(a, LANES - 1, 1), pltpu.roll(b, LANES - 1, 1)
        patch_ref[r, 0:fields, :LANES] = jnp.where(first_lane, columns[:, lane : lane + 1], up_a).astype(BF16)
        patch_ref[r, 0:fields, LANES:] = jnp.where(first_lane, up_a, up_b).astype(BF16)
        patch_ref[r, fields : 2 * fields, :LANES] = a.astype(BF16)
        patch_ref[r, fields : 2 * fields, LANES:] = b.astype(BF16)
        patch_ref[r, 2 * fields :, :LANES] = jnp.where(last_lane, down_b, down_a).astype(BF16)
        patch_ref[r, 2 * fields :, LANES:] = jnp.where(last_lane, columns[:, 64 + lane : 65 + lane], down_b).astype(BF16)

    root = math.sqrt(2.0 / math.pi)
    weight = w_ref[...]
    grad_b = jnp.zeros((channels, COLS), F32)
    grad_l = jnp.zeros((channels, COLS), F32)
    for p in range(pool_rows):
        grad_act = wide_ref[p]
        patch = patch_ref[2 * p : 2 * p + 4].reshape(4 * taps // 3, COLS)
        both = jnp.dot(weight, patch, preferred_element_type=F32)
        act = None
        for k in range(2):
            mask = mask_ref[2 * p + k : 2 * p + k + 1, :]
            v = both[k * channels : (k + 1) * channels] + (bias_ref[...] + land_ref[...] * mask)
            square = v * v
            t = jnp.tanh(v * (root + (root * 0.044715) * square))
            half = 0.5 + 0.5 * t
            gelu = v * half
            slope = half + gelu * (1.0 - t) * (root + (3.0 * root * 0.044715) * square)
            grad_pre = grad_act * slope
            low_ref[p, k * channels : (k + 1) * channels, :] = grad_pre.astype(BF16)
            grad_b += grad_pre
            grad_l += grad_pre * mask
            act = gelu if act is None else act + gelu
        here = pl.ds(p, channels, stride=pool_rows)
        act0[here, :] = act[:, :LANES]
        act1[here, :] = act[:, LANES:]

    pair = (iota((COLS, LANES), 0) // 2 == iota((COLS, LANES), 1)).astype(F32).astype(BF16)
    total = jnp.concatenate([act0[...], act1[...]], axis=1)
    high = total.astype(BF16)
    low = (total - high.astype(F32)).astype(BF16)
    pooled = jnp.dot(high, pair, preferred_element_type=F32) + jnp.dot(low, pair, preferred_element_type=F32)
    pooled_vmem[...] = (pooled * 0.25).astype(BF16).reshape(pooled_vmem.shape)
    copy = pltpu.make_async_copy(pooled_vmem, pooled_ref, sem)
    copy.start()

    grad_w = jnp.zeros((4 * taps // 3, 2 * channels), F32)
    for p in range(pool_rows):
        patch = patch_ref[2 * p : 2 * p + 4].reshape(4 * taps // 3, COLS)
        grad_w += lax.dot_general(patch, low_ref[p], (((1,), (1,)), ((), ())), preferred_element_type=F32)

    ones = jnp.ones((8, COLS), F32)

    def across(grad):
        return lax.dot_general(
            ones, grad, (((1,), (1,)), ((), ())), precision=lax.Precision.HIGHEST, preferred_element_type=F32
        )

    half_taps = taps // 2
    used = half_taps // 8
    grad = grad_w[:taps, :channels] + grad_w[taps // 3 :, channels:]
    sums_ref[0:used] = jnp.concatenate([grad[:half_taps], grad[half_taps:]], axis=1).reshape(used, 8, LANES)
    sums_ref[used] = jnp.concatenate([across(grad_b), across(grad_l)], axis=1)
    sums_ref[used + 1 :] = jnp.zeros((sums_ref.shape[0] - used - 1, 8, LANES), F32)
    copy.wait()


def sum_kernel(x_ref, out_ref):
    out_ref[...] = jnp.broadcast_to(jnp.sum(x_ref[...], axis=0, keepdims=True), out_ref.shape)


def unpack_kernel(x_ref, weight_ref, bias_ref, land_ref):
    half_taps = weight_ref.shape[0] // 2
    channels = weight_ref.shape[1]
    used = half_taps // 8
    both = x_ref[0:used].reshape(half_taps, LANES)
    weight_ref[0:half_taps, :] = both[:, :channels]
    weight_ref[half_taps:, :] = both[:, channels:]
    bias_ref[...] = x_ref[used, 0:1, :channels]
    land_ref[...] = x_ref[used, 0:1, channels:]


def call(kernel, name, outs, *args, scratch=(), scalars=0, places=None, out_places=None, limit=32):
    shapes = [jax.ShapeDtypeStruct(*o) for o in outs]
    single = len(shapes) == 1
    return pl.pallas_call(
        kernel,
        name=name,
        out_shape=shapes[0] if single else shapes,
        in_specs=places or [SMEM] * scalars + [VMEM] * (len(args) - scalars),
        out_specs=out_places or (VMEM if single else [VMEM] * len(shapes)),
        scratch_shapes=list(scratch),
        compiler_params=pltpu.CompilerParams(vmem_limit_bytes=limit * 1024 * 1024),
    )(*args)


def local(fields, weight, bias, land_bias, land_mask, cotangent):
    channels, in_fields = weight.shape[:2]
    taps = 9 * in_fields
    tiles = lax.axis_size(LON)
    rows_count = lax.axis_size(LAT)
    members = lax.axis_size(PLANE)
    pool_rows = ROWS // 2
    columns = fields.shape[2]
    core = lax.axis_index("c").reshape(1)
    factor = 0.25 / math.sqrt(float(cotangent.shape[1] * rows_count * cotangent.shape[2] * tiles))
    field, outer, inner, edges, *prepared = call(
        functools.partial(first_kernel, tiles, factor),
        "first",
        [
            ((ROWS, columns), BF16),
            ((1, columns), BF16),
            ((columns // LANES, LANES), F32),
            ((ROWS, LANES), F32),
            ((2 * channels, 4 * taps // 3), BF16),
            ((channels, COLS), F32),
            ((channels, COLS), F32),
            ((ROWS, COLS), F32),
            ((pool_rows, channels, COLS), F32),
        ],
        core,
        *(
            pltpu.with_memory_space_constraint(given, pltpu.HBM)
            for given in (
                fields[0],
                weight.transpose(2, 3, 1, 0).reshape(taps, channels),
                bias.reshape(1, channels),
                land_bias.reshape(1, channels),
                land_mask,
                cotangent,
            )
        ),
        scratch=[
            pltpu.VMEM((taps, channels), BF16),
            pltpu.VMEM((1, channels), F32),
            pltpu.VMEM((1, channels), F32),
            pltpu.VMEM(land_mask.shape, jnp.int32),
            pltpu.VMEM(cotangent.shape, BF16),
            pltpu.VMEM((channels * pool_rows, LANES), F32),
            pltpu.VMEM((channels * pool_rows, LANES), F32),
            pltpu.SemaphoreType.DMA((6,)),
        ],
        places=[SMEM] + [HBM] * 6,
        limit=32,
    )
    swap = [pair for i in range(1, rows_count - 1, 2) for pair in ((i, i + 1), (i + 1, i))]
    outer = lax.ppermute(outer, LAT, swap)
    inner = lax.all_gather(inner, "c", axis=0, tiled=True)
    pieces = call(
        functools.partial(pack_kernel, tiles),
        "pack",
        [((tiles, PIECE, LANES), BF16)],
        core,
        field,
        outer,
        inner,
        edges,
        scalars=1,
    )
    pieces = lax.all_to_all(pieces, LON, 0, 0, tiled=True)
    pooled, sums = call(
        conv_kernel,
        "conv",
        [(cotangent.shape, BF16), ((members, 8, LANES), F32)],
        pieces,
        *prepared,
        scratch=[
            pltpu.VMEM((in_fields * PIECE, LANES), F32),
            pltpu.VMEM((ROWS + 2, 3 * in_fields, COLS), BF16),
            pltpu.VMEM((pool_rows, 2 * channels, COLS), BF16),
            pltpu.VMEM((channels * pool_rows, LANES), F32),
            pltpu.VMEM((channels * pool_rows, LANES), F32),
            pltpu.VMEM(cotangent.shape, BF16),
            pltpu.SemaphoreType.DMA,
        ],
        out_places=[ANY, VMEM],
    )
    sums = lax.all_to_all(sums, PLANE, 0, 0, tiled=True)
    sums = call(sum_kernel, "sum_plane", [((lax.axis_size("z"), 8, LANES), F32)], sums)
    sums = lax.all_to_all(sums, "z", 0, 0, tiled=True)
    sums = call(sum_kernel, "sum_z", [((members, 8, LANES), F32)], sums)
    sums = lax.all_to_all(sums, PLANE, 0, 0, tiled=True)
    grad_weight, grad_bias, grad_land = call(
        unpack_kernel,
        "unpack",
        [((taps, channels), F32), ((1, channels), F32), ((1, channels), F32)],
        sums,
    )
    grad_weight = grad_weight.reshape(3, 3, in_fields, channels).transpose(3, 2, 0, 1)
    return pooled, grad_weight, grad_bias.reshape(channels), grad_land.reshape(channels)


def solution(mesh):
    physical = Mesh(mesh.devices.reshape(2, 4, 2, 16, 2), AXES)
    placed = (P(LON, LAT, None), P(), P(), P(), P(LAT, LON), P(None, LAT, LON))
    return jax.shard_map(
        local,
        mesh=physical,
        in_specs=placed,
        out_specs=(P(None, LAT, LON), P(), P(), P()),
        check_vma=False,
    )
```

```python
import functools
import math

import jax
import jax.numpy as jnp
from jax import lax
from jax.experimental import pallas as pl
from jax.experimental.pallas import tpu as pltpu
from jax.sharding import Mesh
from jax.sharding import PartitionSpec as P

AXES = ("xh", "y", "c", "z", "xl")
LAT = ("xh", "y", "c")
LON = ("z", "xl")
PLANE = ("xh", "xl", "y", "c")
F32 = jnp.float32
BF16 = jnp.bfloat16
ROWS = 16
COLS = 256
LANES = 128
PIECE = 40
VMEM = pl.BlockSpec(memory_space=pltpu.VMEM)
ANY = pl.BlockSpec(memory_space=pl.ANY)
HBM = pl.BlockSpec(memory_space=pltpu.HBM)
SMEM = pl.BlockSpec(memory_space=pltpu.SMEM)


def iota(shape, dim):
    return lax.broadcasted_iota(jnp.int32, shape, dim)


def edge_lanes(tiles, tile, half):
    if half == 0:
        return 0, 64 + (tile - 1) % tiles
    return LANES - 1, (tile + 1) % tiles


def pack_kernel(tiles, core_ref, x_ref, outer_ref, inner_ref, edges_ref, out_ref):
    first = core_ref[0] == 0
    rows8 = iota((8, LANES), 0)
    lanes = iota((8, LANES), 1)
    beside = jnp.zeros((8, LANES), F32)
    tails = []
    for tile in range(tiles):
        for half in range(2):
            k = 2 * tile + half
            at = pl.ds(k * LANES, LANES)
            out_ref[tile, half * ROWS : (half + 1) * ROWS, :] = x_ref[:, at]
            outer = outer_ref[:, at].astype(F32)
            top = jnp.where(first, outer, inner_ref[k : k + 1, :])
            bottom = jnp.where(first, inner_ref[2 * tiles + k : 2 * tiles + k + 1, :], outer)
            tails.append((top, bottom))
            halo = jnp.where(rows8 == 0, top, jnp.where(rows8 == 1, bottom, 0.0))
            source, target = edge_lanes(tiles, tile, half)
            beside = jnp.where(lanes == target, pltpu.roll(halo, (target - source) % LANES, 1), beside)
    square = jnp.concatenate([edges_ref[...], beside, jnp.zeros((LANES - ROWS - 8, LANES), F32)], axis=0).T
    columns = square[:tiles] + pltpu.roll(square[64 : 64 + tiles], 64, 1)
    for tile in range(tiles):
        (top0, bottom0), (top1, bottom1) = tails[2 * tile : 2 * tile + 2]
        tail = jnp.where(rows8 == 0, top0, 0.0)
        tail = jnp.where(rows8 == 1, top1, tail)
        tail = jnp.where(rows8 == 2, bottom0, tail)
        tail = jnp.where(rows8 == 3, bottom1, tail)
        tail = jnp.where(rows8 == 4, columns[tile : tile + 1], tail)
        out_ref[tile, 2 * ROWS : PIECE, :] = tail.astype(BF16)


def column_of(row, count):
    return jnp.sum(jnp.where(iota((count, count), 0) == iota((count, count), 1), row, 0.0), axis=1, keepdims=True)


def edges_of(tiles, first, x_ref, outer_ref, inner_ref, edges_ref):
    lanes = iota((ROWS, LANES), 1)
    edges = jnp.zeros((ROWS, LANES), F32)
    for k in range(2 * tiles):
        at = pl.ds(k * LANES, LANES)
        block = x_ref[:, at].astype(F32)
        top, bottom = block[0:1], block[ROWS - 1 : ROWS]
        outer_ref[:, at] = jnp.where(first, top, bottom).astype(BF16)
        inner_ref[k : k + 1, :] = jnp.where(first, bottom, top)
        source, target = edge_lanes(tiles, k // 2, k % 2)
        edges = jnp.where(lanes == target, pltpu.roll(block, (target - source) % LANES, 1), edges)
    edges_ref[...] = edges


def first_kernel(
    tiles, core_ref, x_in, w_in, bias_in, land_in, mask_in, cot_in, x_ref, w_ref, bias_ref, land_ref, mask_ref, cot_ref, outer_ref, inner_ref, edges_ref, sems
):
    pairs = [(x_in, x_ref), (cot_in, cot_ref), (w_in, w_ref), (bias_in, bias_ref), (land_in, land_ref), (mask_in, mask_ref)]
    copies = [pltpu.make_async_copy(source, target, sems.at[k]) for k, (source, target) in enumerate(pairs)]
    for copy in copies:
        copy.start()
    copies[0].wait()
    edges_of(tiles, core_ref[0] == 0, x_ref, outer_ref, inner_ref, edges_ref)
    for copy in copies[1:]:
        copy.wait()


def prepare_kernel(factor, w_ref, bias_ref, land_ref, mask_ref, cot_ref, after_ref, w_out, bias_out, land_out, mask_out, wide_out, wide0, wide1):
    del after_ref
    taps, channels = w_ref.shape
    pool_rows = ROWS // 2
    weight = w_ref[...].astype(F32).T
    zero = jnp.zeros((channels, taps // 3), F32)
    upper = jnp.concatenate([weight, zero], axis=1)
    lower = jnp.concatenate([zero, weight], axis=1)
    w_out[...] = jnp.concatenate([upper, lower], axis=0).astype(BF16)
    bias_out[...] = jnp.broadcast_to(column_of(bias_ref[...], channels), bias_out.shape)
    land_out[...] = jnp.broadcast_to(column_of(land_ref[...], channels), land_out.shape)
    mask_out[...] = mask_ref[...].astype(F32)
    spread = (iota((LANES, COLS), 1) // 2 == iota((LANES, COLS), 0)).astype(F32).astype(BF16)
    wide = jnp.dot(cot_ref[...].reshape(channels * pool_rows, LANES), spread, preferred_element_type=F32) * factor
    wide0[...] = wide[:, :LANES]
    wide1[...] = wide[:, LANES:]
    for p in range(pool_rows):
        here = pl.ds(p, channels, stride=pool_rows)
        wide_out[p] = jnp.concatenate([wide0[here, :], wide1[here, :]], axis=1)


def conv_kernel(r_ref, w_ref, bias_ref, land_ref, mask_ref, wide_ref, pooled_ref, sums_ref, flat_ref, patch_ref, low_ref, act0, act1):
    fields = r_ref.shape[0]
    channels = bias_ref.shape[0]
    taps = 9 * fields
    pool_rows = ROWS // 2
    for c in range(fields):
        flat_ref[c * PIECE : (c + 1) * PIECE, :] = r_ref[c].astype(F32)

    def take(k):
        return flat_ref[pl.ds(k, fields, stride=PIECE), :]

    columns = take(36)
    first_lane = iota((fields, LANES), 1) == 0
    last_lane = iota((fields, LANES), 1) == LANES - 1
    for r in range(ROWS + 2):
        if r == 0:
            k0, k1, lane = 32, 33, 16
        elif r == ROWS + 1:
            k0, k1, lane = 34, 35, 17
        else:
            k0, k1, lane = r - 1, ROWS + r - 1, r - 1
        a, b = take(k0), take(k1)
        up_a, up_b = pltpu.roll(a, 1, 1), pltpu.roll(b, 1, 1)
        down_a, down_b = pltpu.roll(a, LANES - 1, 1), pltpu.roll(b, LANES - 1, 1)
        patch_ref[r, 0:fields, :LANES] = jnp.where(first_lane, columns[:, lane : lane + 1], up_a).astype(BF16)
        patch_ref[r, 0:fields, LANES:] = jnp.where(first_lane, up_a, up_b).astype(BF16)
        patch_ref[r, fields : 2 * fields, :LANES] = a.astype(BF16)
        patch_ref[r, fields : 2 * fields, LANES:] = b.astype(BF16)
        patch_ref[r, 2 * fields :, :LANES] = jnp.where(last_lane, down_b, down_a).astype(BF16)
        patch_ref[r, 2 * fields :, LANES:] = jnp.where(last_lane, columns[:, 64 + lane : 65 + lane], down_b).astype(BF16)

    root = math.sqrt(2.0 / math.pi)
    weight = w_ref[...]
    grad_b = jnp.zeros((channels, COLS), F32)
    grad_l = jnp.zeros((channels, COLS), F32)
    for p in range(pool_rows):
        grad_act = wide_ref[p]
        patch = patch_ref[2 * p : 2 * p + 4].reshape(4 * taps // 3, COLS)
        both = jnp.dot(weight, patch, preferred_element_type=F32)
        act = None
        for k in range(2):
            mask = mask_ref[2 * p + k : 2 * p + k + 1, :]
            v = both[k * channels : (k + 1) * channels] + (bias_ref[...] + land_ref[...] * mask)
            square = v * v
            t = jnp.tanh(v * (root + (root * 0.044715) * square))
            half = 0.5 + 0.5 * t
            gelu = v * half
            slope = half + gelu * (1.0 - t) * (root + (3.0 * root * 0.044715) * square)
            grad_pre = grad_act * slope
            low_ref[p, k * channels : (k + 1) * channels, :] = grad_pre.astype(BF16)
            grad_b += grad_pre
            grad_l += grad_pre * mask
            act = gelu if act is None else act + gelu
        here = pl.ds(p, channels, stride=pool_rows)
        act0[here, :] = act[:, :LANES]
        act1[here, :] = act[:, LANES:]

    grad_w = jnp.zeros((4 * taps // 3, 2 * channels), F32)
    for p in range(pool_rows):
        patch = patch_ref[2 * p : 2 * p + 4].reshape(4 * taps // 3, COLS)
        grad_w += lax.dot_general(patch, low_ref[p], (((1,), (1,)), ((), ())), preferred_element_type=F32)

    def across(grad):
        column = jnp.sum(grad, axis=1, keepdims=True)
        eye = iota((channels, channels), 0) == iota((channels, channels), 1)
        return jnp.sum(jnp.where(eye, column, 0.0), axis=0, keepdims=True)

    half_taps = taps // 2
    used = half_taps // 8
    grad = grad_w[:taps, :channels] + grad_w[taps // 3 :, channels:]
    sums_ref[0:used] = jnp.concatenate([grad[:half_taps], grad[half_taps:]], axis=1).reshape(used, 8, LANES)
    sums_ref[used] = jnp.broadcast_to(jnp.concatenate([across(grad_b), across(grad_l)], axis=1), (8, LANES))
    sums_ref[used + 1 :] = jnp.zeros((sums_ref.shape[0] - used - 1, 8, LANES), F32)
    pair = (iota((COLS, LANES), 0) == 2 * iota((COLS, LANES), 1)).astype(F32).astype(BF16)
    halves = [((act[...] + pltpu.roll(act[...], LANES - 1, 1)) * 0.25).astype(BF16) for act in (act0, act1)]
    pooled = jnp.dot(jnp.concatenate(halves, axis=1), pair, preferred_element_type=F32)
    pooled_ref[...] = pooled.astype(BF16).reshape(pooled_ref.shape)


def sum_kernel(x_ref, out_ref):
    out_ref[...] = jnp.broadcast_to(jnp.sum(x_ref[...], axis=0, keepdims=True), out_ref.shape)


def unpack_kernel(x_ref, pooled_ref, weight_out, bias_out, land_out, pooled_out, weight_ref, rows_ref, sems):
    pooled_copy = pltpu.make_async_copy(pooled_ref, pooled_out, sems.at[3])
    pooled_copy.start()
    taps, channels = weight_ref.shape
    half_taps = taps // 2
    used = half_taps // 8
    rows_ref[0:1, :] = x_ref[used, 0:1, :channels]
    rows_ref[8:9, :] = x_ref[used, 0:1, channels:]
    both = x_ref[0:used].reshape(half_taps, LANES)
    weight_ref[0:half_taps, :] = both[:, :channels]
    weight_ref[half_taps:, :] = both[:, channels:]
    pairs = ((weight_ref, weight_out), (rows_ref.at[0:1], bias_out), (rows_ref.at[8:9], land_out))
    copies = [pltpu.make_async_copy(source, target, sems.at[k]) for k, (source, target) in enumerate(pairs)]
    for copy in copies:
        copy.start()
    for copy in copies:
        copy.wait()
    pooled_copy.wait()


def call(kernel, name, outs, *args, scratch=(), scalars=0, places=None, out_places=None, limit=32):
    shapes = [o if isinstance(o, pl.MemoryRef) else jax.ShapeDtypeStruct(*o) for o in outs]
    single = len(shapes) == 1
    return pl.pallas_call(
        kernel,
        name=name,
        out_shape=shapes[0] if single else shapes,
        in_specs=places or [SMEM] * scalars + [VMEM] * (len(args) - scalars),
        out_specs=out_places or (VMEM if single else [VMEM] * len(shapes)),
        scratch_shapes=list(scratch),
        compiler_params=pltpu.CompilerParams(vmem_limit_bytes=limit * 1024 * 1024),
    )(*args)


def local(fields, weight, bias, land_bias, land_mask, cotangent):
    channels, in_fields = weight.shape[:2]
    taps = 9 * in_fields
    tiles = lax.axis_size(LON)
    rows_count = lax.axis_size(LAT)
    members = lax.axis_size(PLANE)
    pool_rows = ROWS // 2
    columns = fields.shape[2]
    core = lax.axis_index("c").reshape(1)
    factor = 0.25 / math.sqrt(float(cotangent.shape[1] * rows_count * cotangent.shape[2] * tiles))
    given = (
        fields[0],
        weight.transpose(2, 3, 1, 0).reshape(taps, channels),
        bias.reshape(1, channels),
        land_bias.reshape(1, channels),
        land_mask,
        cotangent,
    )
    *held, outer, inner, edges = call(
        functools.partial(first_kernel, tiles),
        "first",
        [(array.shape, array.dtype) for array in given]
        + [((1, columns), BF16), ((columns // LANES, LANES), F32), ((ROWS, LANES), F32)],
        core,
        *(pltpu.with_memory_space_constraint(array, pltpu.HBM) for array in given),
        scratch=[pltpu.SemaphoreType.DMA((6,))],
        places=[SMEM] + [HBM] * 6,
    )
    swap = [pair for i in range(1, rows_count - 1, 2) for pair in ((i, i + 1), (i + 1, i))]
    outer = lax.ppermute(outer, LAT, swap)
    inner = lax.all_gather(inner, "c", axis=0, tiled=True)
    after = inner
    prepared = call(
        functools.partial(prepare_kernel, factor),
        "prepare",
        [
            ((2 * channels, 4 * taps // 3), BF16),
            ((channels, COLS), F32),
            ((channels, COLS), F32),
            ((ROWS, COLS), F32),
            ((pool_rows, channels, COLS), F32),
        ],
        *held[1:],
        after,
        scratch=[pltpu.VMEM((channels * pool_rows, LANES), F32)] * 2,
        places=[VMEM] * 5 + [ANY],
    )
    outer, inner, prepared = lax.optimization_barrier((outer, inner, prepared))
    pieces = call(
        functools.partial(pack_kernel, tiles),
        "pack",
        [((tiles, PIECE, LANES), BF16)],
        core,
        held[0],
        outer,
        inner,
        edges,
        scalars=1,
    )
    pieces = lax.all_to_all(pieces, LON, 0, 0, tiled=True)
    pooled, sums = call(
        conv_kernel,
        "conv",
        [pltpu.VMEM(cotangent.shape, BF16), ((members, 8, LANES), F32)],
        pieces,
        *prepared,
        scratch=[
            pltpu.VMEM((in_fields * PIECE, LANES), F32),
            pltpu.VMEM((ROWS + 2, 3 * in_fields, COLS), BF16),
            pltpu.VMEM((pool_rows, 2 * channels, COLS), BF16),
            pltpu.VMEM((channels * pool_rows, LANES), F32),
            pltpu.VMEM((channels * pool_rows, LANES), F32),
        ],
    )
    sums = lax.all_to_all(sums, PLANE, 0, 0, tiled=True)
    sums = call(sum_kernel, "sum_plane", [((lax.axis_size("z"), 8, LANES), F32)], sums)
    sums = lax.all_to_all(sums, "z", 0, 0, tiled=True)
    sums = call(sum_kernel, "sum_z", [((members, 8, LANES), F32)], sums)
    sums = lax.all_to_all(sums, PLANE, 0, 0, tiled=True)
    grad_weight, grad_bias, grad_land, pooled = call(
        unpack_kernel,
        "unpack",
        [((taps, channels), F32), ((1, channels), F32), ((1, channels), F32), (cotangent.shape, BF16)],
        sums,
        pooled,
        scratch=[
            pltpu.VMEM((taps, channels), F32),
            pltpu.VMEM((16, channels), F32),
            pltpu.SemaphoreType.DMA((4,)),
        ],
        out_places=[ANY] * 4,
    )
    grad_weight = grad_weight.reshape(3, 3, in_fields, channels).transpose(3, 2, 0, 1)
    return pooled, grad_weight, grad_bias.reshape(channels), grad_land.reshape(channels)


def solution(mesh):
    physical = Mesh(mesh.devices.reshape(2, 4, 2, 16, 2), AXES)
    placed = (P(LON, LAT, None), P(), P(), P(), P(LAT, LON), P(None, LAT, LON))
    return jax.shard_map(
        local,
        mesh=physical,
        in_specs=placed,
        out_specs=(P(None, LAT, LON), P(), P(), P()),
        check_vma=False,
    )
```

```python
import functools
import math

import jax
import jax.numpy as jnp
from jax import lax
from jax.experimental import pallas as pl
from jax.experimental.pallas import tpu as pltpu
from jax.sharding import Mesh
from jax.sharding import PartitionSpec as P

AXES = ("xh", "y", "c", "z", "xl")
LAT = ("xh", "y", "c")
LON = ("z", "xl")
PLANE = ("xh", "xl", "y", "c")
F32 = jnp.float32
BF16 = jnp.bfloat16
ROWS = 16
COLS = 256
LANES = 128
PIECE = 40
VMEM = pl.BlockSpec(memory_space=pltpu.VMEM)
ANY = pl.BlockSpec(memory_space=pl.ANY)
HBM = pl.BlockSpec(memory_space=pltpu.HBM)
SMEM = pl.BlockSpec(memory_space=pltpu.SMEM)


def iota(shape, dim):
    return lax.broadcasted_iota(jnp.int32, shape, dim)


def turned(index, count):
    return (index + count // 2) % count


def from_far(count, start):
    return [[(i + start) % count for i in range(count)]]


def edge_lanes(tiles, tile, half):
    if half == 0:
        return 0, 64 + (tile - 1) % tiles
    return LANES - 1, (tile + 1) % tiles


def pack_kernel(tiles, core_ref, x_ref, outer_ref, inner_ref, edges_ref, out_ref):
    first = core_ref[0] == 0
    rows8 = iota((8, LANES), 0)
    lanes = iota((8, LANES), 1)
    beside = jnp.zeros((8, LANES), F32)
    tails = []
    for tile in range(tiles):
        for half in range(2):
            k = 2 * tile + half
            at = pl.ds(k * LANES, LANES)
            out_ref[turned(tile, tiles), half * ROWS : (half + 1) * ROWS, :] = x_ref[:, at]
            outer = outer_ref[:, at].astype(F32)
            top = jnp.where(first, outer, inner_ref[k : k + 1, :])
            bottom = jnp.where(first, inner_ref[2 * tiles + k : 2 * tiles + k + 1, :], outer)
            tails.append((top, bottom))
            halo = jnp.where(rows8 == 0, top, jnp.where(rows8 == 1, bottom, 0.0))
            source, target = edge_lanes(tiles, tile, half)
            beside = jnp.where(lanes == target, pltpu.roll(halo, (target - source) % LANES, 1), beside)
    square = jnp.concatenate([edges_ref[...], beside, jnp.zeros((LANES - ROWS - 8, LANES), F32)], axis=0).T
    columns = square[:tiles] + pltpu.roll(square[64 : 64 + tiles], 64, 1)
    for tile in range(tiles):
        (top0, bottom0), (top1, bottom1) = tails[2 * tile : 2 * tile + 2]
        tail = jnp.where(rows8 == 0, top0, 0.0)
        tail = jnp.where(rows8 == 1, top1, tail)
        tail = jnp.where(rows8 == 2, bottom0, tail)
        tail = jnp.where(rows8 == 3, bottom1, tail)
        tail = jnp.where(rows8 == 4, columns[tile : tile + 1], tail)
        out_ref[turned(tile, tiles), 2 * ROWS : PIECE, :] = tail.astype(BF16)


def column_of(row, count):
    return jnp.sum(jnp.where(iota((count, count), 0) == iota((count, count), 1), row, 0.0), axis=1, keepdims=True)


def edges_of(tiles, first, x_ref, outer_ref, inner_ref, edges_ref):
    lanes = iota((ROWS, LANES), 1)
    edges = jnp.zeros((ROWS, LANES), F32)
    for k in range(2 * tiles):
        at = pl.ds(k * LANES, LANES)
        block = x_ref[:, at].astype(F32)
        top, bottom = block[0:1], block[ROWS - 1 : ROWS]
        outer_ref[:, at] = jnp.where(first, top, bottom).astype(BF16)
        inner_ref[k : k + 1, :] = jnp.where(first, bottom, top)
        source, target = edge_lanes(tiles, k // 2, k % 2)
        edges = jnp.where(lanes == target, pltpu.roll(block, (target - source) % LANES, 1), edges)
    edges_ref[...] = edges


def first_kernel(
    tiles, core_ref, x_in, w_in, bias_in, land_in, mask_in, cot_in, x_ref, w_ref, bias_ref, land_ref, mask_ref, cot_ref, outer_ref, inner_ref, edges_ref, sems
):
    pairs = [(x_in, x_ref), (cot_in, cot_ref), (w_in, w_ref), (bias_in, bias_ref), (land_in, land_ref), (mask_in, mask_ref)]
    copies = [pltpu.make_async_copy(source, target, sems.at[k]) for k, (source, target) in enumerate(pairs)]
    for copy in copies:
        copy.start()
    copies[0].wait()
    edges_of(tiles, core_ref[0] == 0, x_ref, outer_ref, inner_ref, edges_ref)
    for copy in copies[1:]:
        copy.wait()


def prepare_kernel(factor, w_ref, bias_ref, land_ref, mask_ref, cot_ref, after_ref, w_out, bias_out, land_out, mask_out, wide_out, wide0, wide1):
    del after_ref
    taps, channels = w_ref.shape
    pool_rows = ROWS // 2
    weight = w_ref[...].astype(F32).T
    zero = jnp.zeros((channels, taps // 3), F32)
    upper = jnp.concatenate([weight, zero], axis=1)
    lower = jnp.concatenate([zero, weight], axis=1)
    w_out[...] = jnp.concatenate([upper, lower], axis=0).astype(BF16)
    bias_out[...] = jnp.broadcast_to(column_of(bias_ref[...], channels), bias_out.shape)
    land_out[...] = jnp.broadcast_to(column_of(land_ref[...], channels), land_out.shape)
    mask_out[...] = mask_ref[...].astype(F32)
    spread = (iota((LANES, COLS), 1) // 2 == iota((LANES, COLS), 0)).astype(F32).astype(BF16)
    wide = jnp.dot(cot_ref[...].reshape(channels * pool_rows, LANES), spread, preferred_element_type=F32) * factor
    wide0[...] = wide[:, :LANES]
    wide1[...] = wide[:, LANES:]
    for p in range(pool_rows):
        here = pl.ds(p, channels, stride=pool_rows)
        wide_out[p] = jnp.concatenate([wide0[here, :], wide1[here, :]], axis=1)


def conv_kernel(r_ref, w_ref, bias_ref, land_ref, mask_ref, wide_ref, pooled_ref, sums_ref, flat_ref, patch_ref, low_ref, act0, act1):
    fields = r_ref.shape[0]
    channels = bias_ref.shape[0]
    taps = 9 * fields
    pool_rows = ROWS // 2
    for c in range(fields):
        flat_ref[c * PIECE : (c + 1) * PIECE, :] = r_ref[turned(c, fields)].astype(F32)

    def take(k):
        return flat_ref[pl.ds(k, fields, stride=PIECE), :]

    columns = take(36)
    first_lane = iota((fields, LANES), 1) == 0
    last_lane = iota((fields, LANES), 1) == LANES - 1
    for r in range(ROWS + 2):
        if r == 0:
            k0, k1, lane = 32, 33, 16
        elif r == ROWS + 1:
            k0, k1, lane = 34, 35, 17
        else:
            k0, k1, lane = r - 1, ROWS + r - 1, r - 1
        a, b = take(k0), take(k1)
        up_a, up_b = pltpu.roll(a, 1, 1), pltpu.roll(b, 1, 1)
        down_a, down_b = pltpu.roll(a, LANES - 1, 1), pltpu.roll(b, LANES - 1, 1)
        patch_ref[r, 0:fields, :LANES] = jnp.where(first_lane, columns[:, lane : lane + 1], up_a).astype(BF16)
        patch_ref[r, 0:fields, LANES:] = jnp.where(first_lane, up_a, up_b).astype(BF16)
        patch_ref[r, fields : 2 * fields, :LANES] = a.astype(BF16)
        patch_ref[r, fields : 2 * fields, LANES:] = b.astype(BF16)
        patch_ref[r, 2 * fields :, :LANES] = jnp.where(last_lane, down_b, down_a).astype(BF16)
        patch_ref[r, 2 * fields :, LANES:] = jnp.where(last_lane, columns[:, 64 + lane : 65 + lane], down_b).astype(BF16)

    root = math.sqrt(2.0 / math.pi)
    weight = w_ref[...]
    grad_b = jnp.zeros((channels, COLS), F32)
    grad_l = jnp.zeros((channels, COLS), F32)
    for p in range(pool_rows):
        grad_act = wide_ref[p]
        patch = patch_ref[2 * p : 2 * p + 4].reshape(4 * taps // 3, COLS)
        both = jnp.dot(weight, patch, preferred_element_type=F32)
        act = None
        for k in range(2):
            mask = mask_ref[2 * p + k : 2 * p + k + 1, :]
            v = both[k * channels : (k + 1) * channels] + (bias_ref[...] + land_ref[...] * mask)
            square = v * v
            t = jnp.tanh(v * (root + (root * 0.044715) * square))
            half = 0.5 + 0.5 * t
            gelu = v * half
            slope = half + gelu * (1.0 - t) * (root + (3.0 * root * 0.044715) * square)
            grad_pre = grad_act * slope
            low_ref[p, k * channels : (k + 1) * channels, :] = grad_pre.astype(BF16)
            grad_b += grad_pre
            grad_l += grad_pre * mask
            act = gelu if act is None else act + gelu
        here = pl.ds(p, channels, stride=pool_rows)
        act0[here, :] = act[:, :LANES]
        act1[here, :] = act[:, LANES:]

    grad_w = jnp.zeros((4 * taps // 3, 2 * channels), F32)
    for p in range(pool_rows):
        patch = patch_ref[2 * p : 2 * p + 4].reshape(4 * taps // 3, COLS)
        grad_w += lax.dot_general(patch, low_ref[p], (((1,), (1,)), ((), ())), preferred_element_type=F32)

    def across(grad):
        column = jnp.sum(grad, axis=1, keepdims=True)
        eye = iota((channels, channels), 0) == iota((channels, channels), 1)
        return jnp.sum(jnp.where(eye, column, 0.0), axis=0, keepdims=True)

    half_taps = taps // 2
    used = half_taps // 8
    grad = grad_w[:taps, :channels] + grad_w[taps // 3 :, channels:]
    sums_ref[0:used] = jnp.concatenate([grad[:half_taps], grad[half_taps:]], axis=1).reshape(used, 8, LANES)
    sums_ref[used] = jnp.broadcast_to(jnp.concatenate([across(grad_b), across(grad_l)], axis=1), (8, LANES))
    sums_ref[used + 1 :] = jnp.zeros((sums_ref.shape[0] - used - 1, 8, LANES), F32)
    pair = (iota((COLS, LANES), 0) == 2 * iota((COLS, LANES), 1)).astype(F32).astype(BF16)
    halves = [((act[...] + pltpu.roll(act[...], LANES - 1, 1)) * 0.25).astype(BF16) for act in (act0, act1)]
    pooled = jnp.dot(jnp.concatenate(halves, axis=1), pair, preferred_element_type=F32)
    pooled_ref[...] = pooled.astype(BF16).reshape(pooled_ref.shape)


def sum_kernel(x_ref, out_ref):
    out_ref[...] = jnp.broadcast_to(jnp.sum(x_ref[...], axis=0, keepdims=True), out_ref.shape)


def unpack_kernel(x_ref, pooled_ref, weight_out, bias_out, land_out, pooled_out, weight_ref, rows_ref, sems):
    pooled_copy = pltpu.make_async_copy(pooled_ref, pooled_out, sems.at[3])
    pooled_copy.start()
    taps, channels = weight_ref.shape
    half_taps = taps // 2
    used = half_taps // 8
    rows_ref[0:1, :] = x_ref[used, 0:1, :channels]
    rows_ref[8:9, :] = x_ref[used, 0:1, channels:]
    both = x_ref[0:used].reshape(half_taps, LANES)
    weight_ref[0:half_taps, :] = both[:, :channels]
    weight_ref[half_taps:, :] = both[:, channels:]
    pairs = ((weight_ref, weight_out), (rows_ref.at[0:1], bias_out), (rows_ref.at[8:9], land_out))
    copies = [pltpu.make_async_copy(source, target, sems.at[k]) for k, (source, target) in enumerate(pairs)]
    for copy in copies:
        copy.start()
    for copy in copies:
        copy.wait()
    pooled_copy.wait()


def call(kernel, name, outs, *args, scratch=(), scalars=0, places=None, out_places=None, limit=32):
    shapes = [o if isinstance(o, pl.MemoryRef) else jax.ShapeDtypeStruct(*o) for o in outs]
    single = len(shapes) == 1
    return pl.pallas_call(
        kernel,
        name=name,
        out_shape=shapes[0] if single else shapes,
        in_specs=places or [SMEM] * scalars + [VMEM] * (len(args) - scalars),
        out_specs=out_places or (VMEM if single else [VMEM] * len(shapes)),
        scratch_shapes=list(scratch),
        compiler_params=pltpu.CompilerParams(vmem_limit_bytes=limit * 1024 * 1024),
    )(*args)


def local(fields, weight, bias, land_bias, land_mask, cotangent):
    channels, in_fields = weight.shape[:2]
    taps = 9 * in_fields
    tiles = lax.axis_size(LON)
    rows_count = lax.axis_size(LAT)
    members = lax.axis_size(PLANE)
    pool_rows = ROWS // 2
    columns = fields.shape[2]
    core = lax.axis_index("c").reshape(1)
    factor = 0.25 / math.sqrt(float(cotangent.shape[1] * rows_count * cotangent.shape[2] * tiles))
    given = (
        fields[0],
        weight.transpose(2, 3, 1, 0).reshape(taps, channels),
        bias.reshape(1, channels),
        land_bias.reshape(1, channels),
        land_mask,
        cotangent,
    )
    *held, outer, inner, edges = call(
        functools.partial(first_kernel, tiles),
        "first",
        [(array.shape, array.dtype) for array in given]
        + [((1, columns), BF16), ((columns // LANES, LANES), F32), ((ROWS, LANES), F32)],
        core,
        *(pltpu.with_memory_space_constraint(array, pltpu.HBM) for array in given),
        scratch=[pltpu.SemaphoreType.DMA((6,))],
        places=[SMEM] + [HBM] * 6,
    )
    swap = [pair for i in range(1, rows_count - 1, 2) for pair in ((i, i + 1), (i + 1, i))]
    outer = lax.ppermute(outer, LAT, swap)
    inner = lax.all_gather(inner, "c", axis=0, tiled=True)
    after = inner
    prepared = call(
        functools.partial(prepare_kernel, factor),
        "prepare",
        [
            ((2 * channels, 4 * taps // 3), BF16),
            ((channels, COLS), F32),
            ((channels, COLS), F32),
            ((ROWS, COLS), F32),
            ((pool_rows, channels, COLS), F32),
        ],
        *held[1:],
        after,
        scratch=[pltpu.VMEM((channels * pool_rows, LANES), F32)] * 2,
        places=[VMEM] * 5 + [ANY],
    )
    outer, inner, prepared = lax.optimization_barrier((outer, inner, prepared))
    pieces = call(
        functools.partial(pack_kernel, tiles),
        "pack",
        [((tiles, PIECE, LANES), BF16)],
        core,
        held[0],
        outer,
        inner,
        edges,
        scalars=1,
    )
    pieces = lax.all_to_all(pieces, LON, 0, 0, tiled=True, axis_index_groups=from_far(tiles, tiles // 2))
    pooled, sums = call(
        conv_kernel,
        "conv",
        [pltpu.VMEM(cotangent.shape, BF16), ((members, 8, LANES), F32)],
        pieces,
        *prepared,
        scratch=[
            pltpu.VMEM((in_fields * PIECE, LANES), F32),
            pltpu.VMEM((ROWS + 2, 3 * in_fields, COLS), BF16),
            pltpu.VMEM((pool_rows, 2 * channels, COLS), BF16),
            pltpu.VMEM((channels * pool_rows, LANES), F32),
            pltpu.VMEM((channels * pool_rows, LANES), F32),
        ],
    )
    plane = from_far(members, members // 2 + lax.axis_size("y") // 2 * lax.axis_size("c"))
    depth = lax.axis_size("z")
    sums = lax.all_to_all(sums, PLANE, 0, 0, tiled=True, axis_index_groups=plane)
    sums = call(sum_kernel, "sum_plane", [((depth, 8, LANES), F32)], sums)
    sums = lax.all_to_all(sums, "z", 0, 0, tiled=True, axis_index_groups=from_far(depth, depth // 2))
    sums = call(sum_kernel, "sum_z", [((members, 8, LANES), F32)], sums)
    sums = lax.all_to_all(sums, PLANE, 0, 0, tiled=True, axis_index_groups=plane)
    grad_weight, grad_bias, grad_land, pooled = call(
        unpack_kernel,
        "unpack",
        [((taps, channels), F32), ((1, channels), F32), ((1, channels), F32), (cotangent.shape, BF16)],
        sums,
        pooled,
        scratch=[
            pltpu.VMEM((taps, channels), F32),
            pltpu.VMEM((16, channels), F32),
            pltpu.SemaphoreType.DMA((4,)),
        ],
        out_places=[ANY] * 4,
    )
    grad_weight = grad_weight.reshape(3, 3, in_fields, channels).transpose(3, 2, 0, 1)
    return pooled, grad_weight, grad_bias.reshape(channels), grad_land.reshape(channels)


def solution(mesh):
    physical = Mesh(mesh.devices.reshape(2, 4, 2, 16, 2), AXES)
    placed = (P(LON, LAT, None), P(), P(), P(), P(LAT, LON), P(None, LAT, LON))
    return jax.shard_map(
        local,
        mesh=physical,
        in_specs=placed,
        out_specs=(P(None, LAT, LON), P(), P(), P()),
        check_vma=False,
    )
```

```python
import functools
import math

import jax
import jax.numpy as jnp
from jax import lax
from jax.experimental import pallas as pl
from jax.experimental.pallas import tpu as pltpu
from jax.sharding import Mesh
from jax.sharding import PartitionSpec as P

AXES = ("xh", "y", "c", "z", "xl")
LAT = ("xh", "y", "c")
LON = ("z", "xl")
PLANE = ("xh", "xl", "y", "c")
F32 = jnp.float32
BF16 = jnp.bfloat16
ROWS = 16
COLS = 256
LANES = 128
PIECE = 40
VMEM = pl.BlockSpec(memory_space=pltpu.VMEM)
ANY = pl.BlockSpec(memory_space=pl.ANY)
HBM = pl.BlockSpec(memory_space=pltpu.HBM)
SMEM = pl.BlockSpec(memory_space=pltpu.SMEM)


def iota(shape, dim):
    return lax.broadcasted_iota(jnp.int32, shape, dim)


def turned(index, count):
    return (index - far_lon(count)) % count


def far_lon(count):
    return count // 2 + 2


def from_far(count, start):
    return [[(i + start) % count for i in range(count)]]


def edge_lanes(tiles, tile, half):
    if half == 0:
        return 0, 64 + (tile - 1) % tiles
    return LANES - 1, (tile + 1) % tiles


def pack_kernel(tiles, core_ref, x_ref, outer_ref, inner_ref, edges_ref, out_ref):
    first = core_ref[0] == 0
    rows8 = iota((8, LANES), 0)
    lanes = iota((8, LANES), 1)
    beside = jnp.zeros((8, LANES), F32)
    tails = []
    for tile in range(tiles):
        for half in range(2):
            k = 2 * tile + half
            at = pl.ds(k * LANES, LANES)
            out_ref[turned(tile, tiles), half * ROWS : (half + 1) * ROWS, :] = x_ref[:, at]
            outer = outer_ref[:, at].astype(F32)
            top = jnp.where(first, outer, inner_ref[k : k + 1, :])
            bottom = jnp.where(first, inner_ref[2 * tiles + k : 2 * tiles + k + 1, :], outer)
            tails.append((top, bottom))
            halo = jnp.where(rows8 == 0, top, jnp.where(rows8 == 1, bottom, 0.0))
            source, target = edge_lanes(tiles, tile, half)
            beside = jnp.where(lanes == target, pltpu.roll(halo, (target - source) % LANES, 1), beside)
    square = jnp.concatenate([edges_ref[...], beside, jnp.zeros((LANES - ROWS - 8, LANES), F32)], axis=0).T
    columns = square[:tiles] + pltpu.roll(square[64 : 64 + tiles], 64, 1)
    for tile in range(tiles):
        (top0, bottom0), (top1, bottom1) = tails[2 * tile : 2 * tile + 2]
        tail = jnp.where(rows8 == 0, top0, 0.0)
        tail = jnp.where(rows8 == 1, top1, tail)
        tail = jnp.where(rows8 == 2, bottom0, tail)
        tail = jnp.where(rows8 == 3, bottom1, tail)
        tail = jnp.where(rows8 == 4, columns[tile : tile + 1], tail)
        out_ref[turned(tile, tiles), 2 * ROWS : PIECE, :] = tail.astype(BF16)


def column_of(row, count):
    return jnp.sum(jnp.where(iota((count, count), 0) == iota((count, count), 1), row, 0.0), axis=1, keepdims=True)


def edges_of(tiles, first, x_ref, outer_ref, inner_ref, edges_ref):
    lanes = iota((ROWS, LANES), 1)
    edges = jnp.zeros((ROWS, LANES), F32)
    for k in range(2 * tiles):
        at = pl.ds(k * LANES, LANES)
        block = x_ref[:, at].astype(F32)
        top, bottom = block[0:1], block[ROWS - 1 : ROWS]
        outer_ref[:, at] = jnp.where(first, top, bottom).astype(BF16)
        inner_ref[k : k + 1, :] = jnp.where(first, bottom, top)
        source, target = edge_lanes(tiles, k // 2, k % 2)
        edges = jnp.where(lanes == target, pltpu.roll(block, (target - source) % LANES, 1), edges)
    edges_ref[...] = edges


def first_kernel(
    tiles, core_ref, x_in, w_in, bias_in, land_in, mask_in, cot_in, x_ref, w_ref, bias_ref, land_ref, mask_ref, cot_ref, outer_ref, inner_ref, edges_ref, sems
):
    pairs = [(x_in, x_ref), (cot_in, cot_ref), (w_in, w_ref), (bias_in, bias_ref), (land_in, land_ref), (mask_in, mask_ref)]
    copies = [pltpu.make_async_copy(source, target, sems.at[k]) for k, (source, target) in enumerate(pairs)]
    for copy in copies:
        copy.start()
    copies[0].wait()
    edges_of(tiles, core_ref[0] == 0, x_ref, outer_ref, inner_ref, edges_ref)
    for copy in copies[1:]:
        copy.wait()


def prepare_kernel(factor, w_ref, bias_ref, land_ref, mask_ref, cot_ref, after_ref, w_out, bias_out, land_out, mask_out, wide_out, wide0, wide1):
    del after_ref
    taps, channels = w_ref.shape
    pool_rows = ROWS // 2
    weight = w_ref[...].astype(F32).T
    zero = jnp.zeros((channels, taps // 3), F32)
    upper = jnp.concatenate([weight, zero], axis=1)
    lower = jnp.concatenate([zero, weight], axis=1)
    w_out[...] = jnp.concatenate([upper, lower], axis=0).astype(BF16)
    bias_out[...] = jnp.broadcast_to(column_of(bias_ref[...], channels), bias_out.shape)
    land_out[...] = jnp.broadcast_to(column_of(land_ref[...], channels), land_out.shape)
    mask_out[...] = mask_ref[...].astype(F32)
    spread = (iota((LANES, COLS), 1) // 2 == iota((LANES, COLS), 0)).astype(F32).astype(BF16)
    wide = jnp.dot(cot_ref[...].reshape(channels * pool_rows, LANES), spread, preferred_element_type=F32) * factor
    wide0[...] = wide[:, :LANES]
    wide1[...] = wide[:, LANES:]
    for p in range(pool_rows):
        here = pl.ds(p, channels, stride=pool_rows)
        wide_out[p] = jnp.concatenate([wide0[here, :], wide1[here, :]], axis=1)


def conv_kernel(r_ref, w_ref, bias_ref, land_ref, mask_ref, wide_ref, pooled_ref, sums_ref, flat_ref, patch_ref, low_ref, act0, act1):
    fields = r_ref.shape[0]
    channels = bias_ref.shape[0]
    taps = 9 * fields
    pool_rows = ROWS // 2
    for c in range(fields):
        flat_ref[c * PIECE : (c + 1) * PIECE, :] = r_ref[turned(c, fields)].astype(F32)

    def take(k):
        return flat_ref[pl.ds(k, fields, stride=PIECE), :]

    columns = take(36)
    first_lane = iota((fields, LANES), 1) == 0
    last_lane = iota((fields, LANES), 1) == LANES - 1
    for r in range(ROWS + 2):
        if r == 0:
            k0, k1, lane = 32, 33, 16
        elif r == ROWS + 1:
            k0, k1, lane = 34, 35, 17
        else:
            k0, k1, lane = r - 1, ROWS + r - 1, r - 1
        a, b = take(k0), take(k1)
        up_a, up_b = pltpu.roll(a, 1, 1), pltpu.roll(b, 1, 1)
        down_a, down_b = pltpu.roll(a, LANES - 1, 1), pltpu.roll(b, LANES - 1, 1)
        patch_ref[r, 0:fields, :LANES] = jnp.where(first_lane, columns[:, lane : lane + 1], up_a).astype(BF16)
        patch_ref[r, 0:fields, LANES:] = jnp.where(first_lane, up_a, up_b).astype(BF16)
        patch_ref[r, fields : 2 * fields, :LANES] = a.astype(BF16)
        patch_ref[r, fields : 2 * fields, LANES:] = b.astype(BF16)
        patch_ref[r, 2 * fields :, :LANES] = jnp.where(last_lane, down_b, down_a).astype(BF16)
        patch_ref[r, 2 * fields :, LANES:] = jnp.where(last_lane, columns[:, 64 + lane : 65 + lane], down_b).astype(BF16)

    root = math.sqrt(2.0 / math.pi)
    weight = w_ref[...]
    grad_b = jnp.zeros((channels, COLS), F32)
    grad_l = jnp.zeros((channels, COLS), F32)
    for p in range(pool_rows):
        grad_act = wide_ref[p]
        patch = patch_ref[2 * p : 2 * p + 4].reshape(4 * taps // 3, COLS)
        both = jnp.dot(weight, patch, preferred_element_type=F32)
        act = None
        for k in range(2):
            mask = mask_ref[2 * p + k : 2 * p + k + 1, :]
            v = both[k * channels : (k + 1) * channels] + (bias_ref[...] + land_ref[...] * mask)
            square = v * v
            t = jnp.tanh(v * (root + (root * 0.044715) * square))
            half = 0.5 + 0.5 * t
            gelu = v * half
            slope = half + gelu * (1.0 - t) * (root + (3.0 * root * 0.044715) * square)
            grad_pre = grad_act * slope
            low_ref[p, k * channels : (k + 1) * channels, :] = grad_pre.astype(BF16)
            grad_b += grad_pre
            grad_l += grad_pre * mask
            act = gelu if act is None else act + gelu
        here = pl.ds(p, channels, stride=pool_rows)
        act0[here, :] = act[:, :LANES]
        act1[here, :] = act[:, LANES:]

    grad_w = jnp.zeros((4 * taps // 3, 2 * channels), F32)
    for p in range(pool_rows):
        patch = patch_ref[2 * p : 2 * p + 4].reshape(4 * taps // 3, COLS)
        grad_w += lax.dot_general(patch, low_ref[p], (((1,), (1,)), ((), ())), preferred_element_type=F32)

    def across(grad):
        column = jnp.sum(grad, axis=1, keepdims=True)
        eye = iota((channels, channels), 0) == iota((channels, channels), 1)
        return jnp.sum(jnp.where(eye, column, 0.0), axis=0, keepdims=True)

    half_taps = taps // 2
    used = half_taps // 8
    grad = grad_w[:taps, :channels] + grad_w[taps // 3 :, channels:]
    sums_ref[0:used] = jnp.concatenate([grad[:half_taps], grad[half_taps:]], axis=1).reshape(used, 8, LANES)
    sums_ref[used] = jnp.broadcast_to(jnp.concatenate([across(grad_b), across(grad_l)], axis=1), (8, LANES))
    sums_ref[used + 1 :] = jnp.zeros((sums_ref.shape[0] - used - 1, 8, LANES), F32)
    pair = (iota((COLS, LANES), 0) == 2 * iota((COLS, LANES), 1)).astype(F32).astype(BF16)
    halves = [((act[...] + pltpu.roll(act[...], LANES - 1, 1)) * 0.25).astype(BF16) for act in (act0, act1)]
    pooled = jnp.dot(jnp.concatenate(halves, axis=1), pair, preferred_element_type=F32)
    pooled_ref[...] = pooled.astype(BF16).reshape(pooled_ref.shape)


def sum_kernel(x_ref, out_ref):
    out_ref[...] = jnp.broadcast_to(jnp.sum(x_ref[...], axis=0, keepdims=True), out_ref.shape)


def unpack_kernel(x_ref, pooled_ref, weight_out, bias_out, land_out, pooled_out, weight_ref, rows_ref, sems):
    pooled_copy = pltpu.make_async_copy(pooled_ref, pooled_out, sems.at[3])
    pooled_copy.start()
    taps, channels = weight_ref.shape
    half_taps = taps // 2
    used = half_taps // 8
    rows_ref[0:1, :] = x_ref[used, 0:1, :channels]
    rows_ref[8:9, :] = x_ref[used, 0:1, channels:]
    both = x_ref[0:used].reshape(half_taps, LANES)
    weight_ref[0:half_taps, :] = both[:, :channels]
    weight_ref[half_taps:, :] = both[:, channels:]
    pairs = ((weight_ref, weight_out), (rows_ref.at[0:1], bias_out), (rows_ref.at[8:9], land_out))
    copies = [pltpu.make_async_copy(source, target, sems.at[k]) for k, (source, target) in enumerate(pairs)]
    for copy in copies:
        copy.start()
    for copy in copies:
        copy.wait()
    pooled_copy.wait()


def call(kernel, name, outs, *args, scratch=(), scalars=0, places=None, out_places=None, limit=32):
    shapes = [o if isinstance(o, pl.MemoryRef) else jax.ShapeDtypeStruct(*o) for o in outs]
    single = len(shapes) == 1
    return pl.pallas_call(
        kernel,
        name=name,
        out_shape=shapes[0] if single else shapes,
        in_specs=places or [SMEM] * scalars + [VMEM] * (len(args) - scalars),
        out_specs=out_places or (VMEM if single else [VMEM] * len(shapes)),
        scratch_shapes=list(scratch),
        compiler_params=pltpu.CompilerParams(vmem_limit_bytes=limit * 1024 * 1024),
    )(*args)


def local(fields, weight, bias, land_bias, land_mask, cotangent):
    channels, in_fields = weight.shape[:2]
    taps = 9 * in_fields
    tiles = lax.axis_size(LON)
    rows_count = lax.axis_size(LAT)
    members = lax.axis_size(PLANE)
    pool_rows = ROWS // 2
    columns = fields.shape[2]
    core = lax.axis_index("c").reshape(1)
    factor = 0.25 / math.sqrt(float(cotangent.shape[1] * rows_count * cotangent.shape[2] * tiles))
    given = (
        fields[0],
        weight.transpose(2, 3, 1, 0).reshape(taps, channels),
        bias.reshape(1, channels),
        land_bias.reshape(1, channels),
        land_mask,
        cotangent,
    )
    *held, outer, inner, edges = call(
        functools.partial(first_kernel, tiles),
        "first",
        [(array.shape, array.dtype) for array in given]
        + [((1, columns), BF16), ((columns // LANES, LANES), F32), ((ROWS, LANES), F32)],
        core,
        *(pltpu.with_memory_space_constraint(array, pltpu.HBM) for array in given),
        scratch=[pltpu.SemaphoreType.DMA((6,))],
        places=[SMEM] + [HBM] * 6,
    )
    swap = [pair for i in range(1, rows_count - 1, 2) for pair in ((i, i + 1), (i + 1, i))]
    outer = lax.ppermute(outer, LAT, swap)
    inner = lax.all_gather(inner, "c", axis=0, tiled=True)
    after = inner
    prepared = call(
        functools.partial(prepare_kernel, factor),
        "prepare",
        [
            ((2 * channels, 4 * taps // 3), BF16),
            ((channels, COLS), F32),
            ((channels, COLS), F32),
            ((ROWS, COLS), F32),
            ((pool_rows, channels, COLS), F32),
        ],
        *held[1:],
        after,
        scratch=[pltpu.VMEM((channels * pool_rows, LANES), F32)] * 2,
        places=[VMEM] * 5 + [ANY],
    )
    outer, inner, prepared = lax.optimization_barrier((outer, inner, prepared))
    pieces = call(
        functools.partial(pack_kernel, tiles),
        "pack",
        [((tiles, PIECE, LANES), BF16)],
        core,
        held[0],
        outer,
        inner,
        edges,
        scalars=1,
    )
    pieces = lax.all_to_all(pieces, LON, 0, 0, tiled=True, axis_index_groups=from_far(tiles, far_lon(tiles)))
    pooled, sums = call(
        conv_kernel,
        "conv",
        [pltpu.VMEM(cotangent.shape, BF16), ((members, 8, LANES), F32)],
        pieces,
        *prepared,
        scratch=[
            pltpu.VMEM((in_fields * PIECE, LANES), F32),
            pltpu.VMEM((ROWS + 2, 3 * in_fields, COLS), BF16),
            pltpu.VMEM((pool_rows, 2 * channels, COLS), BF16),
            pltpu.VMEM((channels * pool_rows, LANES), F32),
            pltpu.VMEM((channels * pool_rows, LANES), F32),
        ],
    )
    plane = from_far(members, members // 2 + lax.axis_size("y") // 2 * lax.axis_size("c") + 1)
    depth = lax.axis_size("z")
    sums = lax.all_to_all(sums, PLANE, 0, 0, tiled=True, axis_index_groups=plane)
    sums = call(sum_kernel, "sum_plane", [((depth, 8, LANES), F32)], sums)
    sums = lax.all_to_all(sums, "z", 0, 0, tiled=True, axis_index_groups=from_far(depth, depth // 2))
    sums = call(sum_kernel, "sum_z", [((members, 8, LANES), F32)], sums)
    sums = lax.all_to_all(sums, PLANE, 0, 0, tiled=True, axis_index_groups=plane)
    grad_weight, grad_bias, grad_land, pooled = call(
        unpack_kernel,
        "unpack",
        [((taps, channels), F32), ((1, channels), F32), ((1, channels), F32), (cotangent.shape, BF16)],
        sums,
        pooled,
        scratch=[
            pltpu.VMEM((taps, channels), F32),
            pltpu.VMEM((16, channels), F32),
            pltpu.SemaphoreType.DMA((4,)),
        ],
        out_places=[ANY] * 4,
    )
    grad_weight = grad_weight.reshape(3, 3, in_fields, channels).transpose(3, 2, 0, 1)
    return pooled, grad_weight, grad_bias.reshape(channels), grad_land.reshape(channels)


def solution(mesh):
    physical = Mesh(mesh.devices.reshape(2, 4, 2, 16, 2), AXES)
    placed = (P(LON, LAT, None), P(), P(), P(), P(LAT, LON), P(None, LAT, LON))
    return jax.shard_map(
        local,
        mesh=physical,
        in_specs=placed,
        out_specs=(P(None, LAT, LON), P(), P(), P()),
        check_vma=False,
    )
```

```python
import functools
import math

import jax
import jax.numpy as jnp
from jax import lax
from jax.experimental import pallas as pl
from jax.experimental.pallas import tpu as pltpu
from jax.sharding import Mesh
from jax.sharding import PartitionSpec as P

AXES = ("xh", "y", "c", "z", "xl")
LAT = ("xh", "y", "c")
LON = ("z", "xl")
PLANE = ("xh", "xl", "y", "c")
F32 = jnp.float32
BF16 = jnp.bfloat16
ROWS = 16
COLS = 256
LANES = 128
PIECE = 40
VMEM = pl.BlockSpec(memory_space=pltpu.VMEM)
ANY = pl.BlockSpec(memory_space=pl.ANY)
HBM = pl.BlockSpec(memory_space=pltpu.HBM)
SMEM = pl.BlockSpec(memory_space=pltpu.SMEM)


def iota(shape, dim):
    return lax.broadcasted_iota(jnp.int32, shape, dim)


def turned(index, count):
    return (index - far_lon(count)) % count


def far_lon(count):
    return count // 2 + 2


def from_far(count, start):
    return [[(i + start) % count for i in range(count)]]


def edge_lanes(tiles, tile, half):
    if half == 0:
        return 0, 64 + (tile - 1) % tiles
    return LANES - 1, (tile + 1) % tiles


def pack_kernel(tiles, core_ref, x_ref, outer_ref, inner_ref, edges_ref, out_ref):
    first = core_ref[0] == 0
    rows8 = iota((8, LANES), 0)
    lanes = iota((8, LANES), 1)
    beside = jnp.zeros((8, LANES), F32)
    tails = []
    for tile in range(tiles):
        for half in range(2):
            k = 2 * tile + half
            at = pl.ds(k * LANES, LANES)
            out_ref[turned(tile, tiles), half * ROWS : (half + 1) * ROWS, :] = x_ref[:, at]
            outer = outer_ref[:, at].astype(F32)
            top = jnp.where(first, outer, inner_ref[k : k + 1, :])
            bottom = jnp.where(first, inner_ref[2 * tiles + k : 2 * tiles + k + 1, :], outer)
            tails.append((top, bottom))
            halo = jnp.where(rows8 == 0, top, jnp.where(rows8 == 1, bottom, 0.0))
            source, target = edge_lanes(tiles, tile, half)
            beside = jnp.where(lanes == target, pltpu.roll(halo, (target - source) % LANES, 1), beside)
    square = jnp.concatenate([edges_ref[...], beside, jnp.zeros((LANES - ROWS - 8, LANES), F32)], axis=0).T
    columns = square[:tiles] + pltpu.roll(square[64 : 64 + tiles], 64, 1)
    for tile in range(tiles):
        (top0, bottom0), (top1, bottom1) = tails[2 * tile : 2 * tile + 2]
        tail = jnp.where(rows8 == 0, top0, 0.0)
        tail = jnp.where(rows8 == 1, top1, tail)
        tail = jnp.where(rows8 == 2, bottom0, tail)
        tail = jnp.where(rows8 == 3, bottom1, tail)
        tail = jnp.where(rows8 == 4, columns[tile : tile + 1], tail)
        out_ref[turned(tile, tiles), 2 * ROWS : PIECE, :] = tail.astype(BF16)


def column_of(row, count):
    return jnp.sum(jnp.where(iota((count, count), 0) == iota((count, count), 1), row, 0.0), axis=1, keepdims=True)


def edges_of(tiles, first, x_ref, outer_ref, inner_ref, edges_ref):
    lanes = iota((ROWS, LANES), 1)
    edges = jnp.zeros((ROWS, LANES), F32)
    for k in range(2 * tiles):
        at = pl.ds(k * LANES, LANES)
        block = x_ref[:, at].astype(F32)
        top, bottom = block[0:1], block[ROWS - 1 : ROWS]
        outer_ref[:, at] = jnp.where(first, top, bottom).astype(BF16)
        inner_ref[k : k + 1, :] = jnp.where(first, bottom, top)
        source, target = edge_lanes(tiles, k // 2, k % 2)
        edges = jnp.where(lanes == target, pltpu.roll(block, (target - source) % LANES, 1), edges)
    edges_ref[...] = edges


def first_kernel(
    tiles, core_ref, x_in, w_in, bias_in, land_in, mask_in, cot_in, x_ref, w_ref, bias_ref, land_ref, mask_ref, cot_ref, outer_ref, inner_ref, edges_ref, sems
):
    pairs = [(x_in, x_ref), (cot_in, cot_ref), (w_in, w_ref), (bias_in, bias_ref), (land_in, land_ref), (mask_in, mask_ref)]
    copies = [pltpu.make_async_copy(source, target, sems.at[k]) for k, (source, target) in enumerate(pairs)]
    for copy in copies:
        copy.start()
    copies[0].wait()
    edges_of(tiles, core_ref[0] == 0, x_ref, outer_ref, inner_ref, edges_ref)
    for copy in copies[1:]:
        copy.wait()


def prepare_kernel(factor, w_ref, bias_ref, land_ref, mask_ref, cot_ref, after_ref, w_out, bias_out, land_out, mask_out, wide_out, wide0, wide1):
    del after_ref
    taps, channels = w_ref.shape
    pool_rows = ROWS // 2
    weight = w_ref[...].astype(F32).T
    zero = jnp.zeros((channels, taps // 3), F32)
    upper = jnp.concatenate([weight, zero], axis=1)
    lower = jnp.concatenate([zero, weight], axis=1)
    w_out[...] = jnp.concatenate([upper, lower], axis=0).astype(BF16)
    bias_out[...] = jnp.broadcast_to(column_of(bias_ref[...], channels), bias_out.shape)
    land_out[...] = jnp.broadcast_to(column_of(land_ref[...], channels), land_out.shape)
    mask_out[...] = mask_ref[...].astype(F32)
    spread = (iota((LANES, COLS), 1) // 2 == iota((LANES, COLS), 0)).astype(F32).astype(BF16)
    wide = jnp.dot(cot_ref[...].reshape(channels * pool_rows, LANES), spread, preferred_element_type=F32) * factor
    wide0[0 : channels * pool_rows, :] = wide[:, :LANES]
    wide1[0 : channels * pool_rows, :] = wide[:, LANES:]
    for p in range(pool_rows):
        here = pl.ds(p, channels, stride=pool_rows)
        wide_out[p] = jnp.concatenate([wide0[here, :], wide1[here, :]], axis=1)


def conv_kernel(r_ref, w_ref, bias_ref, land_ref, mask_ref, wide_ref, pooled_ref, sums_ref, flat_ref, patch_ref, low_ref, act0, act1):
    fields = r_ref.shape[0]
    channels = bias_ref.shape[0]
    taps = 9 * fields
    pool_rows = ROWS // 2
    for c in range(fields):
        flat_ref[c * PIECE : (c + 1) * PIECE, :] = r_ref[turned(c, fields)].astype(F32)

    def take(k):
        return flat_ref[pl.ds(k, fields, stride=PIECE), :]

    columns = take(36)
    first_lane = iota((fields, LANES), 1) == 0
    last_lane = iota((fields, LANES), 1) == LANES - 1
    for r in range(ROWS + 2):
        if r == 0:
            k0, k1, lane = 32, 33, 16
        elif r == ROWS + 1:
            k0, k1, lane = 34, 35, 17
        else:
            k0, k1, lane = r - 1, ROWS + r - 1, r - 1
        a, b = take(k0), take(k1)
        up_a, up_b = pltpu.roll(a, 1, 1), pltpu.roll(b, 1, 1)
        down_a, down_b = pltpu.roll(a, LANES - 1, 1), pltpu.roll(b, LANES - 1, 1)
        patch_ref[r, 0:fields, :LANES] = jnp.where(first_lane, columns[:, lane : lane + 1], up_a).astype(BF16)
        patch_ref[r, 0:fields, LANES:] = jnp.where(first_lane, up_a, up_b).astype(BF16)
        patch_ref[r, fields : 2 * fields, :LANES] = a.astype(BF16)
        patch_ref[r, fields : 2 * fields, LANES:] = b.astype(BF16)
        patch_ref[r, 2 * fields :, :LANES] = jnp.where(last_lane, down_b, down_a).astype(BF16)
        patch_ref[r, 2 * fields :, LANES:] = jnp.where(last_lane, columns[:, 64 + lane : 65 + lane], down_b).astype(BF16)

    root = math.sqrt(2.0 / math.pi)
    weight = w_ref[...]
    grad_b = jnp.zeros((channels, COLS), F32)
    grad_l = jnp.zeros((channels, COLS), F32)
    for p in range(pool_rows):
        grad_act = wide_ref[p]
        patch = patch_ref[2 * p : 2 * p + 4].reshape(4 * taps // 3, COLS)
        both = jnp.dot(weight, patch, preferred_element_type=F32)
        act = None
        for k in range(2):
            mask = mask_ref[2 * p + k : 2 * p + k + 1, :]
            v = both[k * channels : (k + 1) * channels] + (bias_ref[...] + land_ref[...] * mask)
            square = v * v
            t = jnp.tanh(v * (root + (root * 0.044715) * square))
            half = 0.5 + 0.5 * t
            gelu = v * half
            slope = half + gelu * (1.0 - t) * (root + (3.0 * root * 0.044715) * square)
            grad_pre = grad_act * slope
            low_ref[p, k * channels : (k + 1) * channels, :] = grad_pre.astype(BF16)
            grad_b += grad_pre
            grad_l += grad_pre * mask
            act = gelu if act is None else act + gelu
        here = pl.ds(p, channels, stride=pool_rows)
        act0[here, :] = act[:, :LANES]
        act1[here, :] = act[:, LANES:]

    grad_w = jnp.zeros((4 * taps // 3, 2 * channels), F32)
    for p in range(pool_rows):
        patch = patch_ref[2 * p : 2 * p + 4].reshape(4 * taps // 3, COLS)
        grad_w += lax.dot_general(patch, low_ref[p], (((1,), (1,)), ((), ())), preferred_element_type=F32)

    def across(grad):
        column = jnp.sum(grad, axis=1, keepdims=True)
        eye = iota((channels, channels), 0) == iota((channels, channels), 1)
        return jnp.sum(jnp.where(eye, column, 0.0), axis=0, keepdims=True)

    half_taps = taps // 2
    used = half_taps // 8
    grad = grad_w[:taps, :channels] + grad_w[taps // 3 :, channels:]
    sums_ref[0:used] = jnp.concatenate([grad[:half_taps], grad[half_taps:]], axis=1).reshape(used, 8, LANES)
    sums_ref[used] = jnp.broadcast_to(jnp.concatenate([across(grad_b), across(grad_l)], axis=1), (8, LANES))
    sums_ref[used + 1 :] = jnp.zeros((sums_ref.shape[0] - used - 1, 8, LANES), F32)
    pair = (iota((COLS, LANES), 0) == 2 * iota((COLS, LANES), 1)).astype(F32).astype(BF16)
    sums = [act[0 : channels * pool_rows, :] for act in (act0, act1)]
    halves = [((two + pltpu.roll(two, LANES - 1, 1)) * 0.25).astype(BF16) for two in sums]
    pooled = jnp.dot(jnp.concatenate(halves, axis=1), pair, preferred_element_type=F32)
    pooled_ref[...] = pooled.astype(BF16).reshape(pooled_ref.shape)


def sum_kernel(x_ref, out_ref):
    out_ref[...] = jnp.broadcast_to(jnp.sum(x_ref[...], axis=0, keepdims=True), out_ref.shape)


def unpack_kernel(x_ref, pooled_ref, weight_out, bias_out, land_out, pooled_out, weight_ref, rows_ref, sems):
    pooled_copy = pltpu.make_async_copy(pooled_ref, pooled_out, sems.at[3])
    pooled_copy.start()
    taps, channels = weight_ref.shape
    half_taps = taps // 2
    used = half_taps // 8
    rows_ref[0:1, :] = x_ref[used, 0:1, :channels]
    rows_ref[8:9, :] = x_ref[used, 0:1, channels:]
    both = x_ref[0:used].reshape(half_taps, LANES)
    weight_ref[0:half_taps, :] = both[:, :channels]
    weight_ref[half_taps:, :] = both[:, channels:]
    pairs = ((weight_ref, weight_out), (rows_ref.at[0:1], bias_out), (rows_ref.at[8:9], land_out))
    copies = [pltpu.make_async_copy(source, target, sems.at[k]) for k, (source, target) in enumerate(pairs)]
    for copy in copies:
        copy.start()
    for copy in copies:
        copy.wait()
    pooled_copy.wait()


def call(kernel, name, outs, *args, scratch=(), scalars=0, places=None, out_places=None, limit=32):
    shapes = [o if isinstance(o, pl.MemoryRef) else jax.ShapeDtypeStruct(*o) for o in outs]
    single = len(shapes) == 1
    return pl.pallas_call(
        kernel,
        name=name,
        out_shape=shapes[0] if single else shapes,
        in_specs=places or [SMEM] * scalars + [VMEM] * (len(args) - scalars),
        out_specs=out_places or (VMEM if single else [VMEM] * len(shapes)),
        scratch_shapes=list(scratch),
        compiler_params=pltpu.CompilerParams(vmem_limit_bytes=limit * 1024 * 1024),
    )(*args)


def local(fields, weight, bias, land_bias, land_mask, cotangent):
    channels, in_fields = weight.shape[:2]
    taps = 9 * in_fields
    tiles = lax.axis_size(LON)
    rows_count = lax.axis_size(LAT)
    members = lax.axis_size(PLANE)
    pool_rows = ROWS // 2
    columns = fields.shape[2]
    core = lax.axis_index("c").reshape(1)
    factor = 0.25 / math.sqrt(float(cotangent.shape[1] * rows_count * cotangent.shape[2] * tiles))
    given = (
        fields[0],
        weight.transpose(2, 3, 1, 0).reshape(taps, channels),
        bias.reshape(1, channels),
        land_bias.reshape(1, channels),
        land_mask,
        cotangent,
    )
    *held, outer, inner, edges = call(
        functools.partial(first_kernel, tiles),
        "first",
        [(array.shape, array.dtype) for array in given]
        + [((1, columns), BF16), ((columns // LANES, LANES), F32), ((ROWS, LANES), F32)],
        core,
        *(pltpu.with_memory_space_constraint(array, pltpu.HBM) for array in given),
        scratch=[pltpu.SemaphoreType.DMA((6,))],
        places=[SMEM] + [HBM] * 6,
    )
    swap = [pair for i in range(1, rows_count - 1, 2) for pair in ((i, i + 1), (i + 1, i))]
    outer = lax.ppermute(outer, LAT, swap)
    inner = lax.all_gather(inner, "c", axis=0, tiled=True)
    after = inner
    prepared = call(
        functools.partial(prepare_kernel, factor),
        "prepare",
        [
            ((2 * channels, 4 * taps // 3), BF16),
            ((channels, COLS), F32),
            ((channels, COLS), F32),
            ((ROWS, COLS), F32),
            ((pool_rows, channels, COLS), F32),
        ],
        *held[1:],
        after,
        scratch=[pltpu.VMEM(((channels + 1) * pool_rows, LANES), F32)] * 2,
        places=[VMEM] * 5 + [ANY],
    )
    outer, inner, prepared = lax.optimization_barrier((outer, inner, prepared))
    pieces = call(
        functools.partial(pack_kernel, tiles),
        "pack",
        [((tiles, PIECE, LANES), BF16)],
        core,
        held[0],
        outer,
        inner,
        edges,
        scalars=1,
    )
    pieces = lax.all_to_all(pieces, LON, 0, 0, tiled=True, axis_index_groups=from_far(tiles, far_lon(tiles)))
    pooled, sums = call(
        conv_kernel,
        "conv",
        [pltpu.VMEM(cotangent.shape, BF16), ((members, 8, LANES), F32)],
        pieces,
        *prepared,
        scratch=[
            pltpu.VMEM(((in_fields + 1) * PIECE, LANES), F32),
            pltpu.VMEM((ROWS + 2, 3 * in_fields, COLS), BF16),
            pltpu.VMEM((pool_rows, 2 * channels, COLS), BF16),
            pltpu.VMEM(((channels + 1) * pool_rows, LANES), F32),
            pltpu.VMEM(((channels + 1) * pool_rows, LANES), F32),
        ],
    )
    plane = from_far(members, members // 2 + lax.axis_size("y") // 2 * lax.axis_size("c") + 1)
    depth = lax.axis_size("z")
    sums = lax.all_to_all(sums, PLANE, 0, 0, tiled=True, axis_index_groups=plane)
    sums = call(sum_kernel, "sum_plane", [((depth, 8, LANES), F32)], sums)
    sums = lax.all_to_all(sums, "z", 0, 0, tiled=True, axis_index_groups=from_far(depth, depth // 2))
    sums = call(sum_kernel, "sum_z", [((members, 8, LANES), F32)], sums)
    sums = lax.all_to_all(sums, PLANE, 0, 0, tiled=True, axis_index_groups=plane)
    grad_weight, grad_bias, grad_land, pooled = call(
        unpack_kernel,
        "unpack",
        [((taps, channels), F32), ((1, channels), F32), ((1, channels), F32), (cotangent.shape, BF16)],
        sums,
        pooled,
        scratch=[
            pltpu.VMEM((taps, channels), F32),
            pltpu.VMEM((16, channels), F32),
            pltpu.SemaphoreType.DMA((4,)),
        ],
        out_places=[ANY] * 4,
    )
    grad_weight = grad_weight.reshape(3, 3, in_fields, channels).transpose(3, 2, 0, 1)
    return pooled, grad_weight, grad_bias.reshape(channels), grad_land.reshape(channels)


def solution(mesh):
    physical = Mesh(mesh.devices.reshape(2, 4, 2, 16, 2), AXES)
    placed = (P(LON, LAT, None), P(), P(), P(), P(LAT, LON), P(None, LAT, LON))
    return jax.shard_map(
        local,
        mesh=physical,
        in_specs=placed,
        out_specs=(P(None, LAT, LON), P(), P(), P()),
        check_vma=False,
    )
```

```python
import functools
import math

import jax
import jax.numpy as jnp
from jax import lax
from jax.experimental import pallas as pl
from jax.experimental.pallas import tpu as pltpu
from jax.sharding import Mesh
from jax.sharding import PartitionSpec as P

AXES = ("xh", "y", "c", "z", "xl")
LAT = ("xh", "y", "c")
LON = ("z", "xl")
PLANE = ("xh", "xl", "y", "c")
F32 = jnp.float32
BF16 = jnp.bfloat16
ROWS = 16
COLS = 256
LANES = 128
PIECE = 40
VMEM = pl.BlockSpec(memory_space=pltpu.VMEM)
ANY = pl.BlockSpec(memory_space=pl.ANY)
HBM = pl.BlockSpec(memory_space=pltpu.HBM)
SMEM = pl.BlockSpec(memory_space=pltpu.SMEM)


def iota(shape, dim):
    return lax.broadcasted_iota(jnp.int32, shape, dim)


def turned(index, count):
    return (index - far_lon(count)) % count


def far_lon(count):
    return count // 2 + 2


def from_far(count, start):
    return [[(i + start) % count for i in range(count)]]


def edge_lanes(tiles, tile, half):
    if half == 0:
        return 0, 64 + (tile - 1) % tiles
    return LANES - 1, (tile + 1) % tiles


def pack_kernel(tiles, core_ref, x_ref, outer_ref, inner_ref, columns_ref, out_ref):
    first = core_ref[0] == 0
    rows8 = iota((8, LANES), 0)
    last_lane = iota((1, LANES), 1) == LANES - 1
    tops, bottoms = [], []
    for k in range(2 * tiles):
        at = pl.ds(k * LANES, LANES)
        half = k % 2
        out_ref[turned(k // 2, tiles), half * ROWS : (half + 1) * ROWS, :] = x_ref[:, at]
        outer = outer_ref[:, at].astype(F32)
        tops.append(jnp.where(first, outer, inner_ref[k : k + 1, :]))
        bottoms.append(jnp.where(first, inner_ref[2 * tiles + k : 2 * tiles + k + 1, :], outer))
    for tile in range(tiles):
        k = 2 * tile
        before, behind = (k - 1) % (2 * tiles), (k + 2) % (2 * tiles)
        rows = [tops[k], tops[k + 1], bottoms[k], bottoms[k + 1], columns_ref[tile : tile + 1, :]]
        rows += [jnp.where(last_lane, halo[before], halo[behind]) for halo in (tops, bottoms)]
        tail = jnp.zeros((8, LANES), F32)
        for row, values in enumerate(rows):
            tail = jnp.where(rows8 == row, values, tail)
        out_ref[turned(tile, tiles), 2 * ROWS : PIECE, :] = tail.astype(BF16)


def column_of(row, count):
    return jnp.sum(jnp.where(iota((count, count), 0) == iota((count, count), 1), row, 0.0), axis=1, keepdims=True)


def edges_of(tiles, first, x_ref, outer_ref, inner_ref):
    for k in range(2 * tiles):
        at = pl.ds(k * LANES, LANES)
        block = x_ref[:, at].astype(F32)
        top, bottom = block[0:1], block[ROWS - 1 : ROWS]
        outer_ref[:, at] = jnp.where(first, top, bottom).astype(BF16)
        inner_ref[k : k + 1, :] = jnp.where(first, bottom, top)


def columns_of(tiles, x_ref):
    lanes = iota((ROWS, LANES), 1)
    edges = jnp.zeros((ROWS, LANES), F32)
    for k in range(2 * tiles):
        block = x_ref[:, pl.ds(k * LANES, LANES)].astype(F32)
        source, target = edge_lanes(tiles, k // 2, k % 2)
        edges = jnp.where(lanes == target, pltpu.roll(block, (target - source) % LANES, 1), edges)
    square = jnp.concatenate([edges, jnp.zeros((LANES - ROWS, LANES), F32)], axis=0).T
    return square[:tiles] + pltpu.roll(square[64 : 64 + tiles], 64, 1)


def first_kernel(
    tiles, core_ref, x_in, w_in, bias_in, land_in, mask_in, cot_in, x_ref, w_ref, bias_ref, land_ref, mask_ref, cot_ref, outer_ref, inner_ref, sems
):
    pairs = [(x_in, x_ref), (cot_in, cot_ref), (w_in, w_ref), (bias_in, bias_ref), (land_in, land_ref), (mask_in, mask_ref)]
    copies = [pltpu.make_async_copy(source, target, sems.at[k]) for k, (source, target) in enumerate(pairs)]
    for copy in copies:
        copy.start()
    copies[0].wait()
    edges_of(tiles, core_ref[0] == 0, x_ref, outer_ref, inner_ref)
    for copy in copies[1:]:
        copy.wait()


def prepare_kernel(tiles, factor, x_ref, w_ref, bias_ref, land_ref, mask_ref, cot_ref, after_ref, columns_out, w_out, bias_out, land_out, mask_out, wide_out, wide0, wide1):
    del after_ref
    columns_out[...] = columns_of(tiles, x_ref)
    taps, channels = w_ref.shape
    pool_rows = ROWS // 2
    weight = w_ref[...].astype(F32).T
    zero = jnp.zeros((channels, taps // 3), F32)
    upper = jnp.concatenate([weight, zero], axis=1)
    lower = jnp.concatenate([zero, weight], axis=1)
    w_out[...] = jnp.concatenate([upper, lower], axis=0).astype(BF16)
    bias_out[...] = jnp.broadcast_to(column_of(bias_ref[...], channels), bias_out.shape)
    land_out[...] = jnp.broadcast_to(column_of(land_ref[...], channels), land_out.shape)
    mask_out[...] = mask_ref[...].astype(F32)
    spread = (iota((LANES, COLS), 1) // 2 == iota((LANES, COLS), 0)).astype(F32).astype(BF16)
    wide = jnp.dot(cot_ref[...].reshape(channels * pool_rows, LANES), spread, preferred_element_type=F32) * factor
    wide0[0 : channels * pool_rows, :] = wide[:, :LANES]
    wide1[0 : channels * pool_rows, :] = wide[:, LANES:]
    for p in range(pool_rows):
        here = pl.ds(p, channels, stride=pool_rows)
        wide_out[p] = jnp.concatenate([wide0[here, :], wide1[here, :]], axis=1)


def conv_kernel(r_ref, w_ref, bias_ref, land_ref, mask_ref, wide_ref, pooled_ref, sums_ref, flat_ref, patch_ref, low_ref, act0, act1):
    fields = r_ref.shape[0]
    channels = bias_ref.shape[0]
    taps = 9 * fields
    pool_rows = ROWS // 2
    for c in range(fields):
        flat_ref[c * PIECE : (c + 1) * PIECE, :] = r_ref[turned(c, fields)].astype(F32)

    def take(k):
        return flat_ref[pl.ds(k, fields, stride=PIECE), :]

    columns = take(36)
    first_lane = iota((fields, LANES), 1) == 0
    last_lane = iota((fields, LANES), 1) == LANES - 1
    for r in range(ROWS + 2):
        if r == 0:
            k0, k1, sides, left, right = 32, 33, take(37), LANES - 1, 0
        elif r == ROWS + 1:
            k0, k1, sides, left, right = 34, 35, take(38), LANES - 1, 0
        else:
            k0, k1, sides, left, right = r - 1, ROWS + r - 1, columns, r - 1, 63 + r
        a, b = take(k0), take(k1)
        up_a, up_b = pltpu.roll(a, 1, 1), pltpu.roll(b, 1, 1)
        down_a, down_b = pltpu.roll(a, LANES - 1, 1), pltpu.roll(b, LANES - 1, 1)
        patch_ref[r, 0:fields, :LANES] = jnp.where(first_lane, sides[:, left : left + 1], up_a).astype(BF16)
        patch_ref[r, 0:fields, LANES:] = jnp.where(first_lane, up_a, up_b).astype(BF16)
        patch_ref[r, fields : 2 * fields, :LANES] = a.astype(BF16)
        patch_ref[r, fields : 2 * fields, LANES:] = b.astype(BF16)
        patch_ref[r, 2 * fields :, :LANES] = jnp.where(last_lane, down_b, down_a).astype(BF16)
        patch_ref[r, 2 * fields :, LANES:] = jnp.where(last_lane, sides[:, right : right + 1], down_b).astype(BF16)

    root = math.sqrt(2.0 / math.pi)
    weight = w_ref[...]
    grad_b = jnp.zeros((channels, COLS), F32)
    grad_l = jnp.zeros((channels, COLS), F32)
    for p in range(pool_rows):
        grad_act = wide_ref[p]
        patch = patch_ref[2 * p : 2 * p + 4].reshape(4 * taps // 3, COLS)
        both = jnp.dot(weight, patch, preferred_element_type=F32)
        act = None
        for k in range(2):
            mask = mask_ref[2 * p + k : 2 * p + k + 1, :]
            v = both[k * channels : (k + 1) * channels] + (bias_ref[...] + land_ref[...] * mask)
            square = v * v
            t = jnp.tanh(v * (root + (root * 0.044715) * square))
            half = 0.5 + 0.5 * t
            gelu = v * half
            slope = half + gelu * (1.0 - t) * (root + (3.0 * root * 0.044715) * square)
            grad_pre = grad_act * slope
            low_ref[p, k * channels : (k + 1) * channels, :] = grad_pre.astype(BF16)
            grad_b += grad_pre
            grad_l += grad_pre * mask
            act = gelu if act is None else act + gelu
        here = pl.ds(p, channels, stride=pool_rows)
        act0[here, :] = act[:, :LANES]
        act1[here, :] = act[:, LANES:]

    grad_w = jnp.zeros((4 * taps // 3, 2 * channels), F32)
    for p in range(pool_rows):
        patch = patch_ref[2 * p : 2 * p + 4].reshape(4 * taps // 3, COLS)
        grad_w += lax.dot_general(patch, low_ref[p], (((1,), (1,)), ((), ())), preferred_element_type=F32)

    def across(grad):
        column = jnp.sum(grad, axis=1, keepdims=True)
        eye = iota((channels, channels), 0) == iota((channels, channels), 1)
        return jnp.sum(jnp.where(eye, column, 0.0), axis=0, keepdims=True)

    half_taps = taps // 2
    used = half_taps // 8
    grad = grad_w[:taps, :channels] + grad_w[taps // 3 :, channels:]
    sums_ref[0:used] = jnp.concatenate([grad[:half_taps], grad[half_taps:]], axis=1).reshape(used, 8, LANES)
    sums_ref[used] = jnp.broadcast_to(jnp.concatenate([across(grad_b), across(grad_l)], axis=1), (8, LANES))
    sums_ref[used + 1 :] = jnp.zeros((sums_ref.shape[0] - used - 1, 8, LANES), F32)
    pair = (iota((COLS, LANES), 0) == 2 * iota((COLS, LANES), 1)).astype(F32).astype(BF16)
    sums = [act[0 : channels * pool_rows, :] for act in (act0, act1)]
    halves = [((two + pltpu.roll(two, LANES - 1, 1)) * 0.25).astype(BF16) for two in sums]
    pooled = jnp.dot(jnp.concatenate(halves, axis=1), pair, preferred_element_type=F32)
    pooled_ref[...] = pooled.astype(BF16).reshape(pooled_ref.shape)


def sum_kernel(x_ref, out_ref):
    out_ref[...] = jnp.broadcast_to(jnp.sum(x_ref[...], axis=0, keepdims=True), out_ref.shape)


def unpack_kernel(x_ref, pooled_ref, weight_out, bias_out, land_out, pooled_out, weight_ref, rows_ref, sems):
    pooled_copy = pltpu.make_async_copy(pooled_ref, pooled_out, sems.at[3])
    pooled_copy.start()
    taps, channels = weight_ref.shape
    half_taps = taps // 2
    used = half_taps // 8
    rows_ref[0:1, :] = x_ref[used, 0:1, :channels]
    rows_ref[8:9, :] = x_ref[used, 0:1, channels:]
    both = x_ref[0:used].reshape(half_taps, LANES)
    weight_ref[0:half_taps, :] = both[:, :channels]
    weight_ref[half_taps:, :] = both[:, channels:]
    pairs = ((weight_ref, weight_out), (rows_ref.at[0:1], bias_out), (rows_ref.at[8:9], land_out))
    copies = [pltpu.make_async_copy(source, target, sems.at[k]) for k, (source, target) in enumerate(pairs)]
    for copy in copies:
        copy.start()
    for copy in copies:
        copy.wait()
    pooled_copy.wait()


def call(kernel, name, outs, *args, scratch=(), scalars=0, places=None, out_places=None, limit=32):
    shapes = [o if isinstance(o, pl.MemoryRef) else jax.ShapeDtypeStruct(*o) for o in outs]
    single = len(shapes) == 1
    return pl.pallas_call(
        kernel,
        name=name,
        out_shape=shapes[0] if single else shapes,
        in_specs=places or [SMEM] * scalars + [VMEM] * (len(args) - scalars),
        out_specs=out_places or (VMEM if single else [VMEM] * len(shapes)),
        scratch_shapes=list(scratch),
        compiler_params=pltpu.CompilerParams(vmem_limit_bytes=limit * 1024 * 1024),
    )(*args)


def local(fields, weight, bias, land_bias, land_mask, cotangent):
    channels, in_fields = weight.shape[:2]
    taps = 9 * in_fields
    tiles = lax.axis_size(LON)
    rows_count = lax.axis_size(LAT)
    members = lax.axis_size(PLANE)
    pool_rows = ROWS // 2
    columns = fields.shape[2]
    core = lax.axis_index("c").reshape(1)
    factor = 0.25 / math.sqrt(float(cotangent.shape[1] * rows_count * cotangent.shape[2] * tiles))
    given = (
        fields[0],
        weight.transpose(2, 3, 1, 0).reshape(taps, channels),
        bias.reshape(1, channels),
        land_bias.reshape(1, channels),
        land_mask,
        cotangent,
    )
    *held, outer, inner = call(
        functools.partial(first_kernel, tiles),
        "first",
        [(array.shape, array.dtype) for array in given]
        + [((1, columns), BF16), ((columns // LANES, LANES), F32)],
        core,
        *(pltpu.with_memory_space_constraint(array, pltpu.HBM) for array in given),
        scratch=[pltpu.SemaphoreType.DMA((6,))],
        places=[SMEM] + [HBM] * 6,
    )
    swap = [pair for i in range(1, rows_count - 1, 2) for pair in ((i, i + 1), (i + 1, i))]
    outer = lax.ppermute(outer, LAT, swap)
    inner = lax.all_gather(inner, "c", axis=0, tiled=True)
    after = inner
    beside, *prepared = call(
        functools.partial(prepare_kernel, tiles, factor),
        "prepare",
        [
            ((tiles, LANES), F32),
            ((2 * channels, 4 * taps // 3), BF16),
            ((channels, COLS), F32),
            ((channels, COLS), F32),
            ((ROWS, COLS), F32),
            ((pool_rows, channels, COLS), F32),
        ],
        *held,
        after,
        scratch=[pltpu.VMEM(((channels + 1) * pool_rows, LANES), F32)] * 2,
        places=[VMEM] * 6 + [ANY],
    )
    outer, inner, beside, prepared = lax.optimization_barrier((outer, inner, beside, prepared))
    pieces = call(
        functools.partial(pack_kernel, tiles),
        "pack",
        [((tiles, PIECE, LANES), BF16)],
        core,
        held[0],
        outer,
        inner,
        beside,
        scalars=1,
    )
    pieces = lax.all_to_all(pieces, LON, 0, 0, tiled=True, axis_index_groups=from_far(tiles, far_lon(tiles)))
    pooled, sums = call(
        conv_kernel,
        "conv",
        [pltpu.VMEM(cotangent.shape, BF16), ((members, 8, LANES), F32)],
        pieces,
        *prepared,
        scratch=[
            pltpu.VMEM(((in_fields + 1) * PIECE, LANES), F32),
            pltpu.VMEM((ROWS + 2, 3 * in_fields, COLS), BF16),
            pltpu.VMEM((pool_rows, 2 * channels, COLS), BF16),
            pltpu.VMEM(((channels + 1) * pool_rows, LANES), F32),
            pltpu.VMEM(((channels + 1) * pool_rows, LANES), F32),
        ],
    )
    plane = from_far(members, members // 2 + lax.axis_size("y") // 2 * lax.axis_size("c") + 1)
    depth = lax.axis_size("z")
    sums = lax.all_to_all(sums, PLANE, 0, 0, tiled=True, axis_index_groups=plane)
    sums = call(sum_kernel, "sum_plane", [((depth, 8, LANES), F32)], sums)
    sums = lax.all_to_all(sums, "z", 0, 0, tiled=True, axis_index_groups=from_far(depth, depth // 2))
    sums = call(sum_kernel, "sum_z", [((members, 8, LANES), F32)], sums)
    sums = lax.all_to_all(sums, PLANE, 0, 0, tiled=True, axis_index_groups=plane)
    grad_weight, grad_bias, grad_land, pooled = call(
        unpack_kernel,
        "unpack",
        [((taps, channels), F32), ((1, channels), F32), ((1, channels), F32), (cotangent.shape, BF16)],
        sums,
        pooled,
        scratch=[
            pltpu.VMEM((taps, channels), F32),
            pltpu.VMEM((16, channels), F32),
            pltpu.SemaphoreType.DMA((4,)),
        ],
        out_places=[ANY] * 4,
    )
    grad_weight = grad_weight.reshape(3, 3, in_fields, channels).transpose(3, 2, 0, 1)
    return pooled, grad_weight, grad_bias.reshape(channels), grad_land.reshape(channels)


def solution(mesh):
    physical = Mesh(mesh.devices.reshape(2, 4, 2, 16, 2), AXES)
    placed = (P(LON, LAT, None), P(), P(), P(), P(LAT, LON), P(None, LAT, LON))
    return jax.shard_map(
        local,
        mesh=physical,
        in_specs=placed,
        out_specs=(P(None, LAT, LON), P(), P(), P()),
        check_vma=False,
    )
```

```python
import functools
import math

import jax
import jax.numpy as jnp
from jax import lax
from jax.experimental import pallas as pl
from jax.experimental.pallas import tpu as pltpu
from jax.sharding import Mesh
from jax.sharding import PartitionSpec as P

AXES = ("xh", "y", "c", "z", "xl")
LAT = ("xh", "y", "c")
LON = ("z", "xl")
PLANE = ("xh", "xl", "y", "c")
F32 = jnp.float32
BF16 = jnp.bfloat16
ROWS = 16
COLS = 256
LANES = 128
PIECE = 40
VMEM = pl.BlockSpec(memory_space=pltpu.VMEM)
ANY = pl.BlockSpec(memory_space=pl.ANY)
HBM = pl.BlockSpec(memory_space=pltpu.HBM)
SMEM = pl.BlockSpec(memory_space=pltpu.SMEM)


def iota(shape, dim):
    return lax.broadcasted_iota(jnp.int32, shape, dim)


def turned(index, count):
    return (index - far_lon(count)) % count


def far_lon(count):
    return count // 2 + 2


def from_far(count, start):
    return [[(i + start) % count for i in range(count)]]


def edge_lanes(tiles, tile, half):
    if half == 0:
        return 0, 64 + (tile - 1) % tiles
    return LANES - 1, (tile + 1) % tiles


def pack_kernel(tiles, core_ref, x_ref, outer_ref, inner_ref, columns_ref, out_ref):
    first = core_ref[0] == 0
    rows8 = iota((8, LANES), 0)
    last_lane = iota((1, LANES), 1) == LANES - 1
    tops, bottoms = [], []
    for k in range(2 * tiles):
        at = pl.ds(k * LANES, LANES)
        half = k % 2
        out_ref[turned(k // 2, tiles), half * ROWS : (half + 1) * ROWS, :] = x_ref[:, at]
        outer = outer_ref[:, at].astype(F32)
        tops.append(jnp.where(first, outer, inner_ref[k : k + 1, :]))
        bottoms.append(jnp.where(first, inner_ref[2 * tiles + k : 2 * tiles + k + 1, :], outer))
    for tile in range(tiles):
        k = 2 * tile
        before, behind = (k - 1) % (2 * tiles), (k + 2) % (2 * tiles)
        rows = [tops[k], tops[k + 1], bottoms[k], bottoms[k + 1], columns_ref[tile : tile + 1, :]]
        rows += [jnp.where(last_lane, halo[before], halo[behind]) for halo in (tops, bottoms)]
        tail = jnp.zeros((8, LANES), F32)
        for row, values in enumerate(rows):
            tail = jnp.where(rows8 == row, values, tail)
        out_ref[turned(tile, tiles), 2 * ROWS : PIECE, :] = tail.astype(BF16)


def column_of(row, count):
    return jnp.sum(jnp.where(iota((count, count), 0) == iota((count, count), 1), row, 0.0), axis=1, keepdims=True)


def edges_of(tiles, first, x_ref, outer_ref, inner_ref):
    for k in range(2 * tiles):
        at = pl.ds(k * LANES, LANES)
        block = x_ref[:, at].astype(F32)
        top, bottom = block[0:1], block[ROWS - 1 : ROWS]
        outer_ref[:, at] = jnp.where(first, top, bottom).astype(BF16)
        inner_ref[k : k + 1, :] = jnp.where(first, bottom, top)


def columns_of(tiles, x_ref):
    lanes = iota((ROWS, LANES), 1)
    edges = jnp.zeros((ROWS, LANES), F32)
    for k in range(2 * tiles):
        block = x_ref[:, pl.ds(k * LANES, LANES)].astype(F32)
        source, target = edge_lanes(tiles, k // 2, k % 2)
        edges = jnp.where(lanes == target, pltpu.roll(block, (target - source) % LANES, 1), edges)
    square = jnp.concatenate([edges, jnp.zeros((LANES - ROWS, LANES), F32)], axis=0).T
    return square[:tiles] + pltpu.roll(square[64 : 64 + tiles], 64, 1)


def first_kernel(
    tiles, core_ref, x_in, w_in, bias_in, land_in, mask_in, cot_in, x_ref, w_ref, bias_ref, land_ref, mask_ref, cot_ref, outer_ref, inner_ref, sems
):
    pairs = [(x_in, x_ref), (cot_in, cot_ref), (w_in, w_ref), (bias_in, bias_ref), (land_in, land_ref), (mask_in, mask_ref)]
    copies = [pltpu.make_async_copy(source, target, sems.at[k]) for k, (source, target) in enumerate(pairs)]
    for copy in copies:
        copy.start()
    copies[0].wait()
    edges_of(tiles, core_ref[0] == 0, x_ref, outer_ref, inner_ref)
    for copy in copies[1:]:
        copy.wait()


def prepare_kernel(tiles, factor, x_ref, w_ref, bias_ref, land_ref, mask_ref, cot_ref, after_ref, columns_out, w_out, bias_out, land_out, mask_out, wide_out, wide0, wide1):
    del after_ref
    columns_out[...] = columns_of(tiles, x_ref)
    taps, channels = w_ref.shape
    pool_rows = ROWS // 2
    weight = w_ref[...].astype(F32).T
    zero = jnp.zeros((channels, taps // 3), F32)
    upper = jnp.concatenate([weight, zero], axis=1)
    lower = jnp.concatenate([zero, weight], axis=1)
    w_out[...] = jnp.concatenate([upper, lower], axis=0).astype(BF16)
    bias_out[...] = jnp.broadcast_to(column_of(bias_ref[...], channels), bias_out.shape)
    land_out[...] = jnp.broadcast_to(column_of(land_ref[...], channels), land_out.shape)
    mask_out[...] = mask_ref[...].astype(F32)
    spread = (iota((LANES, COLS), 1) // 2 == iota((LANES, COLS), 0)).astype(F32).astype(BF16)
    wide = jnp.dot(cot_ref[...].reshape(channels * pool_rows, LANES), spread, preferred_element_type=F32) * factor
    wide0[0 : channels * pool_rows, :] = wide[:, :LANES]
    wide1[0 : channels * pool_rows, :] = wide[:, LANES:]
    for p in range(pool_rows):
        here = pl.ds(p, channels, stride=pool_rows)
        wide_out[p] = jnp.concatenate([wide0[here, :], wide1[here, :]], axis=1)


def conv_kernel(r_ref, w_ref, bias_ref, land_ref, mask_ref, wide_ref, pooled_ref, sums_ref, flat_ref, patch_ref, low_ref, act0, act1):
    fields = r_ref.shape[0]
    channels = bias_ref.shape[0]
    taps = 9 * fields
    pool_rows = ROWS // 2
    for c in range(fields):
        flat_ref[c * PIECE : (c + 1) * PIECE, :] = r_ref[turned(c, fields)].astype(F32)

    def take(k):
        return flat_ref[pl.ds(k, fields, stride=PIECE), :]

    columns = take(36)
    first_lane = iota((fields, LANES), 1) == 0
    last_lane = iota((fields, LANES), 1) == LANES - 1
    for r in range(ROWS + 2):
        if r == 0:
            k0, k1, sides, left, right = 32, 33, take(37), LANES - 1, 0
        elif r == ROWS + 1:
            k0, k1, sides, left, right = 34, 35, take(38), LANES - 1, 0
        else:
            k0, k1, sides, left, right = r - 1, ROWS + r - 1, columns, r - 1, 63 + r
        a, b = take(k0), take(k1)
        up_a, up_b = pltpu.roll(a, 1, 1), pltpu.roll(b, 1, 1)
        down_a, down_b = pltpu.roll(a, LANES - 1, 1), pltpu.roll(b, LANES - 1, 1)
        patch_ref[r, 0:fields, :LANES] = jnp.where(first_lane, sides[:, left : left + 1], up_a).astype(BF16)
        patch_ref[r, 0:fields, LANES:] = jnp.where(first_lane, up_a, up_b).astype(BF16)
        patch_ref[r, fields : 2 * fields, :LANES] = a.astype(BF16)
        patch_ref[r, fields : 2 * fields, LANES:] = b.astype(BF16)
        patch_ref[r, 2 * fields :, :LANES] = jnp.where(last_lane, down_b, down_a).astype(BF16)
        patch_ref[r, 2 * fields :, LANES:] = jnp.where(last_lane, sides[:, right : right + 1], down_b).astype(BF16)

    root = math.sqrt(2.0 / math.pi)
    weight = w_ref[...]
    grad_b = jnp.zeros((channels, COLS), F32)
    grad_l = jnp.zeros((channels, COLS), F32)
    for p in range(pool_rows):
        grad_act = wide_ref[p]
        patch = patch_ref[2 * p : 2 * p + 4].reshape(4 * taps // 3, COLS)
        both = jnp.dot(weight, patch, preferred_element_type=F32)
        act = None
        for k in range(2):
            mask = mask_ref[2 * p + k : 2 * p + k + 1, :]
            v = both[k * channels : (k + 1) * channels] + (bias_ref[...] + land_ref[...] * mask)
            square = v * v
            t = jnp.tanh(v * (root + (root * 0.044715) * square))
            half = 0.5 + 0.5 * t
            gelu = v * half
            slope = half + gelu * (1.0 - t) * (root + (3.0 * root * 0.044715) * square)
            grad_pre = grad_act * slope
            low_ref[p, k * channels : (k + 1) * channels, :] = grad_pre.astype(BF16)
            grad_b += grad_pre
            grad_l += grad_pre * mask
            act = gelu if act is None else act + gelu
        here = pl.ds(p, channels, stride=pool_rows)
        act0[here, :] = act[:, :LANES]
        act1[here, :] = act[:, LANES:]

    grad_w = jnp.zeros((4 * taps // 3, 2 * channels), F32)
    for p in range(pool_rows):
        patch = patch_ref[2 * p : 2 * p + 4].reshape(4 * taps // 3, COLS)
        grad_w += lax.dot_general(patch, low_ref[p], (((1,), (1,)), ((), ())), preferred_element_type=F32)

    def across(grad):
        column = jnp.sum(grad, axis=1, keepdims=True)
        eye = iota((channels, channels), 0) == iota((channels, channels), 1)
        return jnp.sum(jnp.where(eye, column, 0.0), axis=0, keepdims=True)

    half_taps = taps // 2
    used = half_taps // 8
    grad = grad_w[:taps, :channels] + grad_w[taps // 3 :, channels:]
    sums_ref[0:used] = jnp.concatenate([grad[:half_taps], grad[half_taps:]], axis=1).reshape(used, 8, LANES)
    sums_ref[used] = jnp.broadcast_to(jnp.concatenate([across(grad_b), across(grad_l)], axis=1), (8, LANES))
    sums_ref[used + 1 :] = jnp.zeros((sums_ref.shape[0] - used - 1, 8, LANES), F32)
    pair = (iota((COLS, LANES), 0) == 2 * iota((COLS, LANES), 1)).astype(F32).astype(BF16)
    sums = [act[0 : channels * pool_rows, :] for act in (act0, act1)]
    halves = [((two + pltpu.roll(two, LANES - 1, 1)) * 0.25).astype(BF16) for two in sums]
    pooled = jnp.dot(jnp.concatenate(halves, axis=1), pair, preferred_element_type=F32)
    pooled_ref[...] = pooled.astype(BF16).reshape(pooled_ref.shape)


def sum_kernel(x_ref, out_ref):
    out_ref[...] = jnp.broadcast_to(jnp.sum(x_ref[...], axis=0, keepdims=True).astype(out_ref.dtype), out_ref.shape)


def unpack_kernel(x_ref, pooled_ref, weight_out, bias_out, land_out, pooled_out, weight_ref, rows_ref, sems):
    pooled_copy = pltpu.make_async_copy(pooled_ref, pooled_out, sems.at[3])
    pooled_copy.start()
    taps, channels = weight_ref.shape
    half_taps = taps // 2
    used = half_taps // 8
    sides = x_ref[used].astype(F32)
    rows_ref[0:1, :] = sides[0:1, :channels]
    rows_ref[8:9, :] = sides[0:1, channels:]
    both = x_ref[0:used].astype(F32).reshape(half_taps, LANES)
    weight_ref[0:half_taps, :] = both[:, :channels]
    weight_ref[half_taps:, :] = both[:, channels:]
    pairs = ((weight_ref, weight_out), (rows_ref.at[0:1], bias_out), (rows_ref.at[8:9], land_out))
    copies = [pltpu.make_async_copy(source, target, sems.at[k]) for k, (source, target) in enumerate(pairs)]
    for copy in copies:
        copy.start()
    for copy in copies:
        copy.wait()
    pooled_copy.wait()


def call(kernel, name, outs, *args, scratch=(), scalars=0, places=None, out_places=None, limit=32):
    shapes = [o if isinstance(o, pl.MemoryRef) else jax.ShapeDtypeStruct(*o) for o in outs]
    single = len(shapes) == 1
    return pl.pallas_call(
        kernel,
        name=name,
        out_shape=shapes[0] if single else shapes,
        in_specs=places or [SMEM] * scalars + [VMEM] * (len(args) - scalars),
        out_specs=out_places or (VMEM if single else [VMEM] * len(shapes)),
        scratch_shapes=list(scratch),
        compiler_params=pltpu.CompilerParams(vmem_limit_bytes=limit * 1024 * 1024),
    )(*args)


def local(fields, weight, bias, land_bias, land_mask, cotangent):
    channels, in_fields = weight.shape[:2]
    taps = 9 * in_fields
    tiles = lax.axis_size(LON)
    rows_count = lax.axis_size(LAT)
    members = lax.axis_size(PLANE)
    pool_rows = ROWS // 2
    columns = fields.shape[2]
    core = lax.axis_index("c").reshape(1)
    factor = 0.25 / math.sqrt(float(cotangent.shape[1] * rows_count * cotangent.shape[2] * tiles))
    given = (
        fields[0],
        weight.transpose(2, 3, 1, 0).reshape(taps, channels),
        bias.reshape(1, channels),
        land_bias.reshape(1, channels),
        land_mask,
        cotangent,
    )
    *held, outer, inner = call(
        functools.partial(first_kernel, tiles),
        "first",
        [(array.shape, array.dtype) for array in given]
        + [((1, columns), BF16), ((columns // LANES, LANES), F32)],
        core,
        *(pltpu.with_memory_space_constraint(array, pltpu.HBM) for array in given),
        scratch=[pltpu.SemaphoreType.DMA((6,))],
        places=[SMEM] + [HBM] * 6,
    )
    swap = [pair for i in range(1, rows_count - 1, 2) for pair in ((i, i + 1), (i + 1, i))]
    outer = lax.ppermute(outer, LAT, swap)
    inner = lax.all_gather(inner, "c", axis=0, tiled=True)
    after = inner
    beside, *prepared = call(
        functools.partial(prepare_kernel, tiles, factor),
        "prepare",
        [
            ((tiles, LANES), F32),
            ((2 * channels, 4 * taps // 3), BF16),
            ((channels, COLS), F32),
            ((channels, COLS), F32),
            ((ROWS, COLS), F32),
            ((pool_rows, channels, COLS), F32),
        ],
        *held,
        after,
        scratch=[pltpu.VMEM(((channels + 1) * pool_rows, LANES), F32)] * 2,
        places=[VMEM] * 6 + [ANY],
    )
    outer, inner, beside, prepared = lax.optimization_barrier((outer, inner, beside, prepared))
    pieces = call(
        functools.partial(pack_kernel, tiles),
        "pack",
        [((tiles, PIECE, LANES), BF16)],
        core,
        held[0],
        outer,
        inner,
        beside,
        scalars=1,
    )
    pieces = lax.all_to_all(pieces, LON, 0, 0, tiled=True, axis_index_groups=from_far(tiles, far_lon(tiles)))
    pooled, sums = call(
        conv_kernel,
        "conv",
        [pltpu.VMEM(cotangent.shape, BF16), ((members, 8, LANES), F32)],
        pieces,
        *prepared,
        scratch=[
            pltpu.VMEM(((in_fields + 1) * PIECE, LANES), F32),
            pltpu.VMEM((ROWS + 2, 3 * in_fields, COLS), BF16),
            pltpu.VMEM((pool_rows, 2 * channels, COLS), BF16),
            pltpu.VMEM(((channels + 1) * pool_rows, LANES), F32),
            pltpu.VMEM(((channels + 1) * pool_rows, LANES), F32),
        ],
    )
    plane = from_far(members, members // 2 + lax.axis_size("y") // 2 * lax.axis_size("c") + 1)
    depth = lax.axis_size("z")
    sums = lax.all_to_all(sums, PLANE, 0, 0, tiled=True, axis_index_groups=plane)
    sums = call(sum_kernel, "sum_plane", [((depth, 8, LANES), F32)], sums)
    sums = lax.all_to_all(sums, "z", 0, 0, tiled=True, axis_index_groups=from_far(depth, depth // 2))
    sums = call(sum_kernel, "sum_z", [((members, 8, LANES), BF16)], sums)
    sums = lax.all_to_all(sums, PLANE, 0, 0, tiled=True, axis_index_groups=plane)
    grad_weight, grad_bias, grad_land, pooled = call(
        unpack_kernel,
        "unpack",
        [((taps, channels), F32), ((1, channels), F32), ((1, channels), F32), (cotangent.shape, BF16)],
        sums,
        pooled,
        scratch=[
            pltpu.VMEM((taps, channels), F32),
            pltpu.VMEM((16, channels), F32),
            pltpu.SemaphoreType.DMA((4,)),
        ],
        out_places=[ANY] * 4,
    )
    grad_weight = grad_weight.reshape(3, 3, in_fields, channels).transpose(3, 2, 0, 1)
    return pooled, grad_weight, grad_bias.reshape(channels), grad_land.reshape(channels)


def solution(mesh):
    physical = Mesh(mesh.devices.reshape(2, 4, 2, 16, 2), AXES)
    placed = (P(LON, LAT, None), P(), P(), P(), P(LAT, LON), P(None, LAT, LON))
    return jax.shard_map(
        local,
        mesh=physical,
        in_specs=placed,
        out_specs=(P(None, LAT, LON), P(), P(), P()),
        check_vma=False,
    )
```
